512 devices in a mesh: ctx: 64 (over z, y_lo, core), fsdp: 8 (over y_hi, x).
Axes of the slice: x: 4, y: 8 (y_hi: 2, y_lo: 4; y = y_hi * 4 + y_lo), z: 8, core: 2. Of those that a mesh axis runs over, the one named last changes fastest.
Arguments:
- hidden: bfloat16 [8, 8192, 2560], P('fsdp', 'ctx'), may hold values from -20 to 20
- queries: bfloat16 [8, 8192, 6144], P('fsdp', 'ctx'), may hold values from -6 to 6
- keys: bfloat16 [8, 8192, 512], P('fsdp', 'ctx'), may hold values from -6 to 6
- values: bfloat16 [8, 8192, 512], P('fsdp', 'ctx'), may hold values from -6 to 6
- out_grad: bfloat16 [8, 8192, 6144], P('fsdp', 'ctx'), may hold values from -10 to 10
- doc_ids: int32 [8, 8192], P('fsdp'), may hold values from 0 to 63, never falling along the last dimension, each value on 1 to 129 neighbouring positions
Outputs:
- kv_grads: bfloat16 [8, 8192, 1024], P('fsdp', 'ctx')
- updates: float32 [8, 2560, 128], P('fsdp', 'ctx')
The draws below stay inside these ranges and needn't reach their ends.
Inputs may be any that keep to these rules, and one draw needn't show every extreme that they name: `doc_ids`: in each sequence ids never fall; each run of one id is a document of 1 to 129 positions, and at least one document has 129.
All inputs are finite; a program needn't handle non-finite values.
Results may differ from the reference program's by a relative error of at most 0.0056.
Values may be sent and summed in bfloat16 or wider, within the bound.
A program may use at most 128 MiB of HBM per device.

```python
import math
import jax
import jax.numpy as jnp
import numpy as np
from jax import lax

D = 2560
KV_HEADS = 4
GROUP = 12
HEAD_DIM = 128
TOK_DEV = 128
STEPS = 2
NS_ITERS = 5
BATCH = 8
TOKENS = 8192
DOC_MAX = 129
DOC_COUNT = 64
KV_WIDTH = 512


def draw_hidden(key, part):
    key = jax.random.fold_in(key, 5)
    scale_key, value_key = jax.random.split(key, 2)
    fraction = jnp.arange(D, dtype=jnp.float32) / D
    spread = 10.0 ** jax.random.uniform(scale_key, (D,), jnp.float32)
    fresh_vals = jnp.clip(jax.random.normal(value_key, (BATCH, TOKENS, D), jnp.float32), -4.0, 4.0)
    rise_factor = 3.0 ** (0.5 * fraction)
    return (fresh_vals * spread * rise_factor * 0.25).astype(jnp.bfloat16)


def draw_out_grad(key, part):
    key = jax.random.fold_in(key, 7)
    scale_key, value_key = jax.random.split(key)
    col_count = KV_HEADS * GROUP * HEAD_DIM
    spread = 10.0 ** jax.random.uniform(scale_key, (col_count,), jnp.float32)
    fresh_vals = jnp.clip(jax.random.normal(value_key, (BATCH, TOKENS, col_count), jnp.float32), -4.0, 4.0)
    return (fresh_vals * spread * 0.25).astype(jnp.bfloat16)


def draw_queries(key, part):
    key = jax.random.fold_in(key, 11)
    draw_shape = (BATCH, TOKENS, KV_HEADS, GROUP, HEAD_DIM)
    drawn = jnp.clip(jax.random.normal(key, draw_shape, jnp.float32), -6.0, 6.0)
    return drawn.reshape(BATCH, TOKENS, KV_HEADS * GROUP * HEAD_DIM).astype(jnp.bfloat16)


def draw_keys(key, part):
    key = jax.random.fold_in(key, 13)
    draw_shape = (BATCH, TOKENS, KV_HEADS, HEAD_DIM)
    drawn = jnp.clip(jax.random.normal(key, draw_shape, jnp.float32), -6.0, 6.0)
    return drawn.reshape(BATCH, TOKENS, KV_HEADS * HEAD_DIM).astype(jnp.bfloat16)


def levels(key, dims, cuts, smallest, high):
    gain = 1.0
    for dim, blocks in cuts:
        heights = jax.random.uniform(jax.random.fold_in(jax.random.fold_in(key, 6), dim), (blocks,), jnp.float32, smallest / len(cuts), high / len(cuts))
        gain = gain * jnp.repeat(jnp.exp(heights), dims[dim] // blocks).reshape((-1,) + (1,) * (len(dims) - 1 - dim))
    return gain


def length_profile(amount, total, reach, slope):
    weights = [(1 << 20) // math.isqrt(rank ** slope) + 1 for rank in range(2, amount + 1)]
    rest, given = total - reach - (amount - 1), [1] * (amount - 1)
    while rest > 0:
        candidates = [i for i in range(amount - 1) if given[i] < reach]
        mass, budget = sum([weights[i] for i in candidates]), rest
        for i in candidates:
            addition = min(reach - given[i], max(1, budget * weights[i] // mass), rest)
            given[i] = given[i] + addition
            rest = rest - addition
    return np.array([reach] + given)


def ragged_sizes(key, count, total, bound, lean):
    if count == 2:
        one = jax.random.randint(key, (), max(1, total - bound), min(bound, total - 1) + 1)
        return jnp.stack([one, total - one])
    lengths = jnp.asarray(length_profile(count, total, bound, lean), jnp.int32)
    couples = (count - 1) // 2
    source_of, taker = lengths[1:1 + 2 * couples:2], lengths[2:2 + 2 * couples:2]
    margin = jnp.minimum(source_of - 1, bound - taker)
    shifted = jax.random.randint(jax.random.fold_in(key, 1), (couples,), 0, 1 << 20) % (margin + 1)
    lengths = lengths.at[1:1 + 2 * couples:2].set(source_of - shifted).at[2:2 + 2 * couples:2].set(taker + shifted)
    return lengths[jax.random.permutation(jax.random.fold_in(key, 2), count)]


def centred(key, dims, deviation, most, cuts=(), held_as=jnp.bfloat16):
    result = deviation * jax.random.normal(key, dims, jnp.float32)
    if cuts:
        result = result * levels(key, dims, cuts, -0.22, 0.18)
    return jnp.clip(result, -most, most).astype(held_as)


def setup_inputs(seed: int = 0) -> dict:
    key_of = jax.random.split(jax.random.key(seed), 7)
    hidden = draw_hidden(jax.random.fold_in(key_of[6], 71), 0)
    queries = draw_queries(jax.random.fold_in(key_of[6], 71), 0)
    keys = draw_keys(jax.random.fold_in(key_of[6], 71), 0)
    values = centred(key_of[3], (BATCH, TOKENS, KV_WIDTH), 1.0, 6.0, ((0, 8), (1, 64)))
    out_grad = draw_out_grad(jax.random.fold_in(key_of[6], 71), 0)
    doc_ids = jax.vmap(lambda own: jnp.searchsorted(jnp.cumsum(ragged_sizes(own, DOC_COUNT, TOKENS, DOC_MAX, 2)), jnp.arange(TOKENS), side="right"))(jax.random.split(key_of[5], BATCH)).reshape((BATCH, TOKENS)).astype(jnp.int32)
    return {"hidden": hidden, "queries": queries, "keys": keys, "values": values, "out_grad": out_grad, "doc_ids": doc_ids}


coeff_a = 3.4445
coeff_b = -4.775
coeff_c = 2.0315

def window_mask(query_doc, key_doc, pad_len):
    row_index = lax.broadcasted_iota(jnp.int32, (query_doc.shape[0], key_doc.shape[0]), 0)
    col_index = lax.broadcasted_iota(jnp.int32, (query_doc.shape[0], key_doc.shape[0]), 1)
    same_doc = query_doc[:, None] == key_doc[None, :]
    return jnp.logical_and(same_doc, col_index <= row_index + pad_len)

def group_grads(q_group, g_group, k_group, v_group, visible):
    score_scale = 1.0 / math.sqrt(HEAD_DIM)
    scores = score_scale * jnp.einsum('ihd,jd->hij', q_group.astype(jnp.float32), k_group.astype(jnp.float32))
    masked = jnp.where(visible[None], scores, -1e+30)
    row_max = lax.optimization_barrier(jnp.max(masked, axis=-1, keepdims=True))
    exp_vals = jnp.where(visible[None], jnp.exp(masked - row_max), 0.0)
    attn_probs = exp_vals / lax.optimization_barrier(jnp.sum(exp_vals, axis=-1, keepdims=True))
    prob_grad = jnp.einsum('ihd,jd->hij', g_group.astype(jnp.float32), v_group.astype(jnp.float32))
    row_delta = lax.optimization_barrier(jnp.sum(attn_probs * prob_grad, axis=-1, keepdims=True))
    score_low = lax.optimization_barrier((attn_probs * (prob_grad - row_delta)).astype(jnp.bfloat16)).astype(jnp.float32)
    probs_low = lax.optimization_barrier(attn_probs.astype(jnp.bfloat16)).astype(jnp.float32)
    key_grad = score_scale * jnp.einsum('hij,ihd->jd', score_low, q_group.astype(jnp.float32))
    value_grad = jnp.einsum('hij,ihd->jd', probs_low, g_group.astype(jnp.float32))
    return (key_grad, value_grad)

def sequence_grads(operands):
    q_seq, g_seq, k_seq, v_seq, doc_row = operands
    pad_len = (STEPS - 1) * TOK_DEV
    keys_pad = jnp.concatenate([jnp.zeros((pad_len, k_seq.shape[1]), k_seq.dtype), k_seq], axis=0)
    vals_pad = jnp.concatenate([jnp.zeros((pad_len, v_seq.shape[1]), v_seq.dtype), v_seq], axis=0)
    doc_pad = jnp.concatenate([jnp.full((pad_len,), -1, jnp.int32), doc_row.astype(jnp.int32)], axis=0)
    block_count = TOKENS // TOK_DEV
    kv_cols = 2 * KV_HEADS * HEAD_DIM

    def block_grads(block_idx):
        row_start = (block_idx * TOK_DEV).astype(jnp.int32)
        q_blk = lax.dynamic_slice_in_dim(q_seq, row_start, TOK_DEV, 0).reshape(TOK_DEV, KV_HEADS, GROUP, HEAD_DIM)
        g_blk = lax.dynamic_slice_in_dim(g_seq, row_start, TOK_DEV, 0).reshape(TOK_DEV, KV_HEADS, GROUP, HEAD_DIM)
        k_blk = lax.dynamic_slice_in_dim(keys_pad, row_start, STEPS * TOK_DEV, 0).reshape(STEPS * TOK_DEV, KV_HEADS, HEAD_DIM)
        v_blk = lax.dynamic_slice_in_dim(vals_pad, row_start, STEPS * TOK_DEV, 0).reshape(STEPS * TOK_DEV, KV_HEADS, HEAD_DIM)
        key_doc = lax.dynamic_slice_in_dim(doc_pad, row_start, STEPS * TOK_DEV, 0)
        query_doc = lax.dynamic_slice_in_dim(doc_pad, row_start + pad_len, TOK_DEV, 0)
        visible = window_mask(query_doc, key_doc, pad_len)
        key_parts = []
        value_parts = []
        for head_group in range(KV_HEADS):
            key_grad, value_grad = group_grads(q_blk[:, head_group], g_blk[:, head_group], k_blk[:, head_group], v_blk[:, head_group], visible)
            key_parts.append(key_grad)
            value_parts.append(value_grad)
        joined = jnp.concatenate(key_parts + value_parts, axis=1)
        return joined.reshape(STEPS, TOK_DEV, kv_cols)
    contribs = lax.map(block_grads, jnp.arange(block_count, dtype=jnp.int32))
    totals = jnp.zeros((block_count + STEPS - 1, TOK_DEV, kv_cols), jnp.float32)
    for step_idx in range(STEPS):
        totals = totals.at[step_idx:step_idx + block_count].add(contribs[:, step_idx])
    return totals[STEPS - 1:].reshape(TOKENS, kv_cols).astype(jnp.bfloat16)

def orthogonalize(weight_grad):
    frob_norm = jnp.sqrt(lax.optimization_barrier(jnp.sum(weight_grad * weight_grad, axis=(1, 2), keepdims=True)))
    ns_state = weight_grad / (frob_norm + 1e-07)
    for iteration in range(NS_ITERS):
        ns_gram = jnp.einsum('mrd,mre->mde', ns_state, ns_state, precision=lax.Precision.HIGHEST)
        squared = jnp.einsum('mde,mef->mdf', ns_gram, ns_gram, precision=lax.Precision.HIGHEST)
        poly_term = coeff_b * ns_gram + coeff_c * squared
        ns_state = coeff_a * ns_state + jnp.einsum('mre,mde->mrd', ns_state, poly_term, precision=lax.Precision.HIGHEST)
    return math.sqrt(D) * ns_state

def reference(hidden, queries, keys, values, out_grad, doc_ids):
    kv_grads = lax.map(sequence_grads, (queries, out_grad, keys, values, doc_ids))
    flat_hidden = hidden.reshape(BATCH * TOKENS, D)
    flat_grads = kv_grads.reshape(BATCH * TOKENS, 2 * KV_HEADS * HEAD_DIM)
    weight_grad = jnp.dot(flat_hidden.T, flat_grads, preferred_element_type=jnp.float32)
    weight_grad = weight_grad.reshape(D, 2 * KV_HEADS, HEAD_DIM).transpose(1, 0, 2)
    updates = orthogonalize(weight_grad)
    return (kv_grads, updates)
```

```python
import math

import jax
import jax.numpy as jnp
from jax import lax
from jax.experimental import pallas as pl
from jax.experimental.pallas import tpu as pltpu
from jax.sharding import PartitionSpec as P

D = 2560
KV_HEADS = 4
GROUP = 12
HEAD_DIM = 128
NS_ITERS = 5
TOK = 128
X, Y, Z, YL = 4, 8, 8, 4
QUARTER = D // X
CHUNK = QUARTER // Y
ROWS = CHUNK // 2
HEADS_W = GROUP * HEAD_DIM
KV_W = KV_HEADS * HEAD_DIM

coeff_a = 3.4445
coeff_b = -4.775
coeff_c = 2.0315

F32 = jnp.float32
BF16 = jnp.bfloat16
MESH = pl.DeviceIdType.MESH
HIGHEST = lax.Precision.HIGHEST


def device(x, yh, yl, z, core):
    return {"ctx": z * 8 + yl * 2 + core, "fsdp": yh * 4 + x}


def remote(src, dst, send, recv, to):
    return pltpu.make_async_remote_copy(
        src_ref=src, dst_ref=dst, send_sem=send, recv_sem=recv, device_id=to, device_id_type=MESH
    )


def mm(a, b, dims, **kw):
    return lax.dot_general(a, b, ((dims[0], dims[1]), ((), ())), preferred_element_type=F32, **kw)


def kernel(
    hid, qs, ks, vs, og, docs, kv_out, up_out,
    q_v, g_v, kwin, bias, acck, accv, csend, cown, crecv, kvb, hall, ht, kall, w32, wlo,
    yrecv, zsend, zrecv, gpart, g1buf, s1, g2buf, gfull,
    loc, kvs, kvr, hs, hr, cs, cr, xs, xr, ys, yr, zs, zr, g1s, g1r, g2s, g2r, g3s, g3r, outs,
):
    ctx, fsdp = lax.axis_index("ctx"), lax.axis_index("fsdp")
    z, yl, core = ctx // 8, lax.rem(ctx // 2, YL), lax.rem(ctx, 2)
    yh, x = fsdp // X, lax.rem(fsdp, X)
    y = yh * YL + yl
    other = 1 - core
    nxt, prv = lax.rem(ctx + 1, 64), lax.rem(ctx + 63, 64)

    def load_q(g):
        cols = slice(g * HEADS_W, (g + 1) * HEADS_W)
        return (
            pltpu.make_async_copy(qs.at[0, :, cols], q_v.at[:, cols], loc.at[g]),
            pltpu.make_async_copy(og.at[0, :, cols], g_v.at[:, cols], loc.at[4 + g]),
        )

    own_k = pltpu.make_async_copy(ks.at[0], kwin.at[0, 1], loc.at[8])
    own_v = pltpu.make_async_copy(vs.at[0], kwin.at[1, 1], loc.at[9])
    own_h = pltpu.make_async_copy(hid.at[0, :, pl.ds(pl.multiple_of(x * QUARTER, 128), QUARTER)], hall.at[0], loc.at[10])
    own_k.start()
    own_v.start()
    for g in range(KV_HEADS):
        for c in load_q(g):
            c.start()
    own_h.start()

    cell = yl * 2 + core

    def x_dev(dx, dc):
        return device(lax.rem(x + dx, X), yh, yl, z, lax.rem(core + dc, 2))

    def y_dev(k):
        to = lax.rem(y + k, Y)
        return device(x, to // YL, lax.rem(to, YL), z, core)

    def cell_dev(k):
        to = lax.rem(cell + k, 8)
        return {"ctx": z * 8 + to, "fsdp": fsdp}

    def z_dev(k):
        return {"ctx": lax.rem(z + k, Z) * 8 + cell, "fsdp": fsdp}

    def owner(g, half):
        return device(g, core, yl, 2 * x + yh, half)

    selfish = jnp.logical_and(core == yh, z == 2 * x + yh)
    barrier = pltpu.get_barrier_semaphore()

    def greet(to):
        pl.semaphore_signal(barrier, inc=1, device_id=to, device_id_type=MESH)

    count = 0
    for to in ({"ctx": nxt, "fsdp": fsdp}, {"ctx": prv, "fsdp": fsdp}):
        greet(to)
        count += 1
    for k in range(1, 8):
        greet(x_dev(k // 2, k % 2))
        greet(y_dev(k))
        greet(cell_dev(k))
        greet(z_dev(k))
        count += 4
    for k in range(Z):
        src = device(z // 2, lax.rem(z, 2), yl, lax.rem(z + k, Z), yh)
        if k == 0:
            @pl.when(jnp.logical_not(selfish))
            def _():
                greet(src)
        else:
            greet(src)
        count += 1

    eye = lax.broadcasted_iota(jnp.int32, (TOK, TOK), 0) == lax.broadcasted_iota(jnp.int32, (TOK, TOK), 1)
    own_row = docs[:, pl.ds(pl.multiple_of(ctx * TOK, TOK), TOK)].astype(F32)
    prv_row = docs[:, pl.ds(pl.multiple_of(prv * TOK, TOK), TOK)].astype(F32)
    prv_row = jnp.where(ctx == 0, -1.0, prv_row)

    def as_column(row):
        return jnp.sum(jnp.where(eye, jnp.broadcast_to(row, (TOK, TOK)), 0.0), axis=1, keepdims=True)

    earlier = lax.broadcasted_iota(jnp.int32, (TOK, TOK), 0) <= lax.broadcasted_iota(jnp.int32, (TOK, TOK), 1)
    bias[0:TOK, :] = jnp.where(as_column(prv_row) == own_row, 0.0, -1e30)
    bias[TOK:, :] = jnp.where(jnp.logical_and(as_column(own_row) == own_row, earlier), 0.0, -1e30)

    pl.semaphore_wait(barrier, count - selfish.astype(jnp.int32))

    send_k = remote(ks.at[0], kwin.at[0, 0], kvs.at[0], kvr.at[0], {"ctx": nxt, "fsdp": fsdp})
    send_v = remote(vs.at[0], kwin.at[1, 0], kvs.at[1], kvr.at[1], {"ctx": nxt, "fsdp": fsdp})
    send_k.start()
    send_v.start()

    def hidden_cols(which):
        return hid.at[0, :, pl.ds(pl.multiple_of(which * QUARTER, 128), QUARTER)]

    send_h = [
        remote(hidden_cols(lax.rem(x + dx, X)), hall.at[2 * dx], hs.at[2 * dx], hr.at[2 * dx], x_dev(dx, 0))
        for dx in range(1, X)
    ]
    send_h.append(remote(hidden_cols(x), hall.at[1], hs.at[1], hr.at[1], x_dev(0, 1)))
    for c in send_h:
        c.start()
    forward_h = [
        remote(hall.at[2 * dx], hall.at[2 * dx + 1], hs.at[2 * dx + 1], hr.at[2 * dx + 1], x_dev(0, 1))
        for dx in range(1, X)
    ]

    scale = 1.0 / math.sqrt(HEAD_DIM)
    scale2 = scale * math.log2(math.e)

    def attention(g):
        for c in load_q(g):
            c.wait()
        lanes = slice(g * HEAD_DIM, (g + 1) * HEAD_DIM)
        kw = kwin[0, :, :, lanes].reshape(2 * TOK, HEAD_DIM)
        vw = kwin[1, :, :, lanes].reshape(2 * TOK, HEAD_DIM)
        acck[...] = jnp.zeros_like(acck)
        accv[...] = jnp.zeros_like(accv)

        def pair(i, _):
            at = [pl.ds(pl.multiple_of((g * GROUP + 2 * i + j) * HEAD_DIM, HEAD_DIM), HEAD_DIM) for j in range(2)]
            q2 = jnp.concatenate([q_v[:, at[0]], q_v[:, at[1]]], axis=0)
            g2 = jnp.concatenate([g_v[:, at[0]], g_v[:, at[1]]], axis=0)
            both = jnp.concatenate([bias[...], bias[...]], axis=1)
            s = mm(kw, q2, ((1,), (1,))) * scale2 + both
            dp = mm(vw, g2, ((1,), (1,)))
            e = jnp.exp2(s - jnp.max(s, axis=0, keepdims=True))
            inv = 1.0 / jnp.sum(e, axis=0, keepdims=True)
            p = e * inv
            delta = jnp.sum(p * dp, axis=0, keepdims=True)
            ds = (p * (dp - delta)).astype(BF16)
            acck[...] += mm(ds, q2, ((1,), (0,)))
            accv[...] += mm(p.astype(BF16), g2, ((1,), (0,)))
            return 0

        lax.fori_loop(0, GROUP // 2, pair, 0)
        csend[g, 0] = acck[0:TOK, :] * scale
        csend[g, 1] = accv[0:TOK, :]
        cown[g, 0] = acck[TOK:, :] * scale
        cown[g, 1] = accv[TOK:, :]

    def contribs(g):
        return remote(csend.at[g], crecv.at[g], cs.at[g], cr.at[g], {"ctx": prv, "fsdp": fsdp})

    def x_copies(g):
        return [
            remote(
                kvb.at[g, lax.rem(core + k % 2, 2)], kall.at[g, k], xs.at[g, k], xr.at[g, k], x_dev(k // 2, k % 2)
            )
            for k in (1, 2, 4, 6, 3, 5, 7)
        ]

    def out_copies(g):
        return [
            pltpu.make_async_copy(
                kvb.at[g, j], kv_out.at[0, :, pl.ds(j * KV_W + g * HEAD_DIM, HEAD_DIM)], outs.at[2 * g + j]
            )
            for j in range(2)
        ]

    def finish(g):
        contribs(g).wait_recv()
        kvb[g] = (crecv[g] + cown[g]).astype(BF16)
        for c in x_copies(g):
            c.start()
        kall[g, 0] = kvb[g, core]
        for c in out_copies(g):
            c.start()

    def y_copies(g):
        return [
            remote(wlo.at[g, lax.rem(y + k, Y)], yrecv.at[g, k], ys.at[g, k], yr.at[g, k], y_dev(k))
            for k in (4, 3, 5, 2, 6, 1, 7)
        ]

    def product(g):
        for c in x_copies(g):
            c.wait_recv()
        w = mm(ht[...], kall[g].reshape(8 * TOK, HEAD_DIM), ((1,), (0,))).reshape(Y, CHUNK, HEAD_DIM)
        wlo[g] = w.astype(BF16)
        for c in y_copies(g):
            c.start()
        w32[g] = w

    def z_copy(g, half):
        return remote(zsend.at[g, half], zrecv.at[z], zs.at[g, half], zr.at[z], owner(g, half))

    def z_local(g, half):
        return pltpu.make_async_copy(zsend.at[g, half], zrecv.at[z], zr.at[z])

    def is_mine(g, half):
        return jnp.logical_and(selfish, jnp.logical_and(x == g, core == half))

    def y_sum(g):
        for c in y_copies(g):
            c.wait_recv()
        total = w32[g, y]
        for k in range(1, Y):
            total = total + yrecv[g, k].astype(F32)
        zsend[g] = total.reshape(2, ROWS, HEAD_DIM)
        for half in range(2):
            mine = is_mine(g, half)

            @pl.when(mine)
            def _(half=half):
                z_local(g, half).start()

            @pl.when(jnp.logical_not(mine))
            def _(half=half):
                z_copy(g, half).start()

    own_k.wait()
    own_v.wait()
    send_k.wait_recv()
    send_v.wait_recv()
    attention(0)
    contribs(0).start()
    for c in send_h[:3]:
        c.wait_recv()
    for c in forward_h:
        c.start()
    attention(1)
    contribs(1).start()
    finish(0)
    own_h.wait()
    send_h[3].wait_recv()
    for c in forward_h:
        c.wait_recv()
    for k in range(8):
        ht[:, k * TOK:(k + 1) * TOK] = hall[k].T
    attention(2)
    contribs(2).start()
    finish(1)
    product(0)
    attention(3)
    contribs(3).start()
    finish(2)
    product(1)
    y_sum(0)
    finish(3)
    product(2)
    y_sum(1)
    product(3)
    y_sum(2)
    y_sum(3)

    send_k.wait_send()
    send_v.wait_send()
    for c in send_h + forward_h:
        c.wait_send()
    for g in range(KV_HEADS):
        contribs(g).wait_send()
        for c in x_copies(g) + y_copies(g):
            c.wait_send()
        for c in out_copies(g):
            c.wait()
        for half in range(2):
            @pl.when(jnp.logical_not(is_mine(g, half)))
            def _(half=half):
                z_copy(g, half).wait_send()

    for k in range(Z):
        pltpu.make_async_copy(zrecv.at[k], zrecv.at[k], zr.at[k]).wait()
    w = zrecv[0]
    for k in range(1, Z):
        w = w + zrecv[k]

    gpart[...] = mm(w, w, ((0,), (0,)), precision=HIGHEST).reshape(8, 16, HEAD_DIM)
    step1 = [
        remote(gpart.at[lax.rem(cell + k, 8)], g1buf.at[k], g1s.at[k], g1r.at[k], cell_dev(k)) for k in range(1, 8)
    ]
    for c in step1:
        c.start()
    total = gpart[cell]
    for c in step1:
        c.wait_recv()
    for k in range(1, 8):
        total = total + g1buf[k]
    s1[...] = total
    step2 = [remote(s1, g2buf.at[k], g2s.at[k], g2r.at[k], z_dev(k)) for k in range(1, 8)]
    for c in step2:
        c.start()
    for c in step1:
        c.wait_send()
    for c in step2:
        c.wait_recv()
    for k in range(1, 8):
        total = total + g2buf[k]
    gfull[cell] = total
    step3 = [remote(gfull.at[cell], gfull.at[cell], g3s.at[k], g3r.at[k], cell_dev(k)) for k in range(1, 8)]
    for c in step3:
        c.start()
    for c in step2:
        c.wait_send()
    for c in step3:
        c.wait_recv()
    gram = gfull[...].reshape(HEAD_DIM, HEAD_DIM)

    ident = jnp.where(eye, 1.0, 0.0)
    norm = jnp.sqrt(jnp.sum(jnp.sum(gram * ident, axis=1, keepdims=True), axis=0, keepdims=True))
    inv = 1.0 / (norm + 1e-07)
    gram = gram * inv * inv

    def dot(a, b):
        return mm(a, b, ((1,), (0,)), precision=HIGHEST)

    run = None
    for it in range(NS_ITERS):
        poly = coeff_a * ident + coeff_b * gram + coeff_c * dot(gram, gram)
        run = poly if run is None else dot(run, poly)
        if it < NS_ITERS - 1:
            gram = dot(dot(poly, gram), poly)
    up_out[0] = dot(w * (inv * math.sqrt(D)), run)
    for c in step3:
        c.wait_send()


def shards(hidden, queries, keys, values, out_grad, doc_ids):
    any_spec = pl.BlockSpec(memory_space=pl.ANY)
    vmem = pl.BlockSpec(memory_space=pltpu.VMEM)
    dma = pltpu.SemaphoreType.DMA
    heads = KV_HEADS
    return pl.pallas_call(
        kernel,
        out_shape=(
            jax.ShapeDtypeStruct((1, TOK, 2 * KV_W), BF16),
            jax.ShapeDtypeStruct((1, ROWS, HEAD_DIM), F32),
        ),
        in_specs=[any_spec] * 5 + [vmem],
        out_specs=(any_spec, vmem),
        scratch_shapes=[
            pltpu.VMEM((TOK, heads * HEADS_W), BF16),
            pltpu.VMEM((TOK, heads * HEADS_W), BF16),
            pltpu.VMEM((2, 2, TOK, KV_W), BF16),
            pltpu.VMEM((2 * TOK, TOK), F32),
            pltpu.VMEM((2 * TOK, HEAD_DIM), F32),
            pltpu.VMEM((2 * TOK, HEAD_DIM), F32),
            pltpu.VMEM((heads, 2, TOK, HEAD_DIM), F32),
            pltpu.VMEM((heads, 2, TOK, HEAD_DIM), F32),
            pltpu.VMEM((heads, 2, TOK, HEAD_DIM), F32),
            pltpu.VMEM((heads, 2, TOK, HEAD_DIM), BF16),
            pltpu.VMEM((8, TOK, QUARTER), BF16),
            pltpu.VMEM((QUARTER, 8 * TOK), BF16),
            pltpu.VMEM((heads, 8, TOK, HEAD_DIM), BF16),
            pltpu.VMEM((heads, Y, CHUNK, HEAD_DIM), F32),
            pltpu.VMEM((heads, Y, CHUNK, HEAD_DIM), BF16),
            pltpu.VMEM((heads, Y, CHUNK, HEAD_DIM), BF16),
            pltpu.VMEM((heads, 2, ROWS, HEAD_DIM), F32),
            pltpu.VMEM((Z, ROWS, HEAD_DIM), F32),
            pltpu.VMEM((8, 16, HEAD_DIM), F32),
            pltpu.VMEM((8, 16, HEAD_DIM), F32),
            pltpu.VMEM((16, HEAD_DIM), F32),
            pltpu.VMEM((8, 16, HEAD_DIM), F32),
            pltpu.VMEM((8, 16, HEAD_DIM), F32),
            dma((11,)),
            dma((2,)), dma((2,)),
            dma((8,)), dma((8,)),
            dma((heads,)), dma((heads,)),
            dma((heads, 8)), dma((heads, 8)),
            dma((heads, 8)), dma((heads, 8)),
            dma((heads, 2)), dma((Z,)),
            dma((8,)), dma((8,)),
            dma((8,)), dma((8,)),
            dma((8,)), dma((8,)),
            dma((8,)),
        ],
        compiler_params=pltpu.CompilerParams(
            collective_id=0, has_side_effects=True, vmem_limit_bytes=40 * 1024 * 1024
        ),
        name="muon_kv_grads",
    )(hidden, queries, keys, values, out_grad, doc_ids)


def solution(mesh):
    placed = (P("fsdp", "ctx", None),) * 5 + (P("fsdp", None),)
    return jax.shard_map(
        shards,
        mesh=mesh,
        in_specs=placed,
        out_specs=(P("fsdp", "ctx", None), P("fsdp", "ctx", None)),
        check_vma=False,
    )
```

```python
import math

import jax
import jax.numpy as jnp
from jax import lax
from jax.experimental import pallas as pl
from jax.experimental.pallas import tpu as pltpu
from jax.sharding import PartitionSpec as P

D = 2560
KV_HEADS = 4
GROUP = 12
HEAD_DIM = 128
NS_ITERS = 5
TOK = 128
X, Y, Z, YL = 4, 8, 8, 4
QUARTER = D // X
CHUNK = QUARTER // Y
ROWS = CHUNK // 2
HEADS_W = GROUP * HEAD_DIM
KV_W = KV_HEADS * HEAD_DIM

coeff_a = 3.4445
coeff_b = -4.775
coeff_c = 2.0315

F32 = jnp.float32
BF16 = jnp.bfloat16
MESH = pl.DeviceIdType.MESH
HIGHEST = lax.Precision.HIGHEST


def device(x, yh, yl, z, core):
    return {"ctx": z * 8 + yl * 2 + core, "fsdp": yh * 4 + x}


def remote(src, dst, send, recv, to):
    return pltpu.make_async_remote_copy(
        src_ref=src, dst_ref=dst, send_sem=send, recv_sem=recv, device_id=to, device_id_type=MESH
    )


def mm(a, b, dims, **kw):
    return lax.dot_general(a, b, ((dims[0], dims[1]), ((), ())), preferred_element_type=F32, **kw)


def wait_bytes(ref, sem):
    pltpu.make_async_copy(ref, ref, sem).wait()


def kernel(
    hid, qs, ks, vs, og, docs, kv_out, up_out,
    q_v, g_v, kwin, bias, qst, gst, dsb, pbb, csend, cown, crecv, kvb, hall, ht, kall, w32, wlo,
    yrecv, zsend, zrecv, gpart, g1buf, s1, g2buf, gfull,
    loc, loh, kvs, kvr, hs, hr, cs, cr, xs, xr, ys, yr, zs, zr, g1s, g1r, g2s, g2r, g3s, g3r, outs,
):
    ctx, fsdp = lax.axis_index("ctx"), lax.axis_index("fsdp")
    z, yl, core = ctx // 8, lax.rem(ctx // 2, YL), lax.rem(ctx, 2)
    yh, x = fsdp // X, lax.rem(fsdp, X)
    y = yh * YL + yl
    cell = yl * 2 + core
    nxt, prv = lax.rem(ctx + 1, 64), lax.rem(ctx + 63, 64)

    def x_dev(dx, dc):
        return device(lax.rem(x + dx, X), yh, yl, z, lax.rem(core + dc, 2))

    def y_dev(k):
        to = lax.rem(y + k, Y)
        return device(x, to // YL, lax.rem(to, YL), z, core)

    def cell_dev(k):
        return {"ctx": z * 8 + lax.rem(cell + k, 8), "fsdp": fsdp}

    def z_dev(k):
        return {"ctx": lax.rem(z + k, Z) * 8 + cell, "fsdp": fsdp}

    def owner(g, half):
        return device(g, core, yl, 2 * x + yh, half)

    selfish = jnp.logical_and(core == yh, z == 2 * x + yh)
    barrier = pltpu.get_barrier_semaphore()

    def greet(to):
        pl.semaphore_signal(barrier, inc=1, device_id=to, device_id_type=MESH)

    greet({"ctx": nxt, "fsdp": fsdp})
    greet({"ctx": prv, "fsdp": fsdp})
    for k in range(1, 8):
        greet(x_dev(k % 4, k // 4))
        greet(y_dev(k))
        greet(cell_dev(k))
        greet(z_dev(k))
    sources = [device(z // 2, lax.rem(z, 2), yl, lax.rem(z + k, Z), yh) for k in range(Z)]

    @pl.when(jnp.logical_not(selfish))
    def _():
        greet(sources[0])

    for src in sources[1:]:
        greet(src)
    greeted = 2 + 4 * 7 + Z - selfish.astype(jnp.int32)

    def loads(g):
        wide = slice(g * HEADS_W, (g + 1) * HEADS_W)
        lanes = slice(g * HEAD_DIM, (g + 1) * HEAD_DIM)
        return (
            pltpu.make_async_copy(qs.at[0, :, wide], q_v.at[:, wide], loc.at[g, 0]),
            pltpu.make_async_copy(og.at[0, :, wide], g_v.at[:, wide], loc.at[g, 1]),
            pltpu.make_async_copy(ks.at[0, :, lanes], kwin.at[g, 1, 0], loc.at[g, 2]),
            pltpu.make_async_copy(vs.at[0, :, lanes], kwin.at[g, 1, 1], loc.at[g, 3]),
        )

    def hidden_cols(which):
        return hid.at[0, :, pl.ds(pl.multiple_of(which * QUARTER, 128), QUARTER)]

    own_h = pltpu.make_async_copy(hidden_cols(x), hall.at[0], loh)
    for g in range(KV_HEADS):
        for c in loads(g):
            c.start()
    own_h.start()

    eye = lax.broadcasted_iota(jnp.int32, (TOK, TOK), 0) == lax.broadcasted_iota(jnp.int32, (TOK, TOK), 1)
    own_row = docs[:, pl.ds(pl.multiple_of(ctx * TOK, TOK), TOK)].astype(F32)
    prv_row = docs[:, pl.ds(pl.multiple_of(prv * TOK, TOK), TOK)].astype(F32)
    prv_row = jnp.where(ctx == 0, -1.0, prv_row)

    def as_column(row):
        return jnp.sum(jnp.where(eye, jnp.broadcast_to(row, (TOK, TOK)), 0.0), axis=1, keepdims=True)

    earlier = lax.broadcasted_iota(jnp.int32, (TOK, TOK), 0) <= lax.broadcasted_iota(jnp.int32, (TOK, TOK), 1)
    bias[0:TOK, :] = jnp.where(as_column(prv_row) == own_row, 0.0, -1e30)
    bias[TOK:, :] = jnp.where(jnp.logical_and(as_column(own_row) == own_row, earlier), 0.0, -1e30)

    pl.semaphore_wait(barrier, greeted)

    def window(g):
        lanes = slice(g * HEAD_DIM, (g + 1) * HEAD_DIM)
        to = {"ctx": nxt, "fsdp": fsdp}
        return (
            remote(ks.at[0, :, lanes], kwin.at[g, 0, 0], kvs.at[g], kvr.at[g], to),
            remote(vs.at[0, :, lanes], kwin.at[g, 0, 1], kvs.at[g], kvr.at[g], to),
        )

    for g in range(KV_HEADS):
        for c in window(g):
            c.start()
    for dx in (2, 1, 3):
        remote(hidden_cols(lax.rem(x + dx, X)), hall.at[dx], hs.at[0], hr.at[0], x_dev(dx, 0)).start()
    remote(hidden_cols(x), hall.at[4], hs.at[1], hr.at[1], x_dev(0, 1)).start()

    def forward_hidden():
        wait_bytes(hall.at[1:4], hr.at[0])
        for dx in range(1, X):
            remote(hall.at[dx], hall.at[4 + dx], hs.at[1], hr.at[1], x_dev(0, 1)).start()

    def turn_hidden():
        own_h.wait()
        wait_bytes(hall.at[4:8], hr.at[1])
        for k in range(8):
            ht[:, k * TOK:(k + 1) * TOK] = hall[k].T

    scale = 1.0 / math.sqrt(HEAD_DIM)
    scale2 = scale * math.log2(math.e)

    def contribs(g):
        return remote(csend.at[g], crecv.at[g], cs.at[g], cr.at[g], {"ctx": prv, "fsdp": fsdp})

    def attention(g):
        for c in loads(g):
            c.wait()
        wait_bytes(kwin.at[g, 0], kvr.at[g])
        kw = jnp.concatenate([kwin[g, 0, 0], kwin[g, 1, 0]], axis=0)
        vw = jnp.concatenate([kwin[g, 0, 1], kwin[g, 1, 1]], axis=0)
        both = jnp.concatenate([bias[...], bias[...]], axis=1)
        for i in range(GROUP // 2):
            at = [slice((g * GROUP + 2 * i + j) * HEAD_DIM, (g * GROUP + 2 * i + j + 1) * HEAD_DIM) for j in range(2)]
            q2 = jnp.concatenate([q_v[:, at[0]], q_v[:, at[1]]], axis=0)
            g2 = jnp.concatenate([g_v[:, at[0]], g_v[:, at[1]]], axis=0)
            s = mm(kw, q2, ((1,), (1,))) * scale2 + both
            dp = mm(vw, g2, ((1,), (1,)))
            e = jnp.exp2(s - jnp.max(s, axis=0, keepdims=True))
            inv = 1.0 / jnp.sum(e, axis=0, keepdims=True)
            p = e * inv
            delta = jnp.sum(p * dp, axis=0, keepdims=True)
            cols = slice(2 * i * HEAD_DIM, 2 * (i + 1) * HEAD_DIM)
            dsb[:, cols] = (p * (dp - delta)).astype(BF16)
            pbb[:, cols] = p.astype(BF16)
            qst[cols, :] = q2
            gst[cols, :] = g2
        csend[g, 0] = mm(dsb[0:TOK, :], qst[...], ((1,), (0,))) * scale
        csend[g, 1] = mm(pbb[0:TOK, :], gst[...], ((1,), (0,)))
        contribs(g).start()
        cown[g, 0] = mm(dsb[TOK:, :], qst[...], ((1,), (0,))) * scale
        cown[g, 1] = mm(pbb[TOK:, :], gst[...], ((1,), (0,)))

    def out_copies(g):
        return [
            pltpu.make_async_copy(
                kvb.at[g, j], kv_out.at[0, :, j * KV_W + g * HEAD_DIM:j * KV_W + (g + 1) * HEAD_DIM], outs.at[2 * g + j]
            )
            for j in range(2)
        ]

    def finish(g):
        contribs(g).wait_recv()
        kvb[g] = (crecv[g] + cown[g]).astype(BF16)
        for k in (2, 6, 1, 3, 5, 7, 4):
            remote(
                kvb.at[g, lax.rem(core + k // 4, 2)], kall.at[g, k], xs.at[g], xr.at[g], x_dev(k % 4, k // 4)
            ).start()
        kall[g, 0] = kvb[g, core]
        for c in out_copies(g):
            c.start()

    def product(g):
        wait_bytes(kall.at[g, 1:8], xr.at[g])
        w = mm(ht[...], kall[g].reshape(8 * TOK, HEAD_DIM), ((1,), (0,))).reshape(Y, CHUNK, HEAD_DIM)
        wlo[g] = w.astype(BF16)
        for k in (4, 3, 5, 2, 6, 1, 7):
            remote(wlo.at[g, lax.rem(y + k, Y)], yrecv.at[g, k], ys.at[g], yr.at[g], y_dev(k)).start()
        w32[g] = w

    def z_copy(g, half):
        return remote(zsend.at[g, half], zrecv.at[z], zs.at[g, half], zr, owner(g, half))

    def is_mine(g, half):
        return jnp.logical_and(selfish, jnp.logical_and(x == g, core == half))

    def y_sum(g):
        wait_bytes(yrecv.at[g, 1:8], yr.at[g])
        total = w32[g, y]
        for k in range(1, Y):
            total = total + yrecv[g, k].astype(F32)
        zsend[g] = total.reshape(2, ROWS, HEAD_DIM)
        for half in range(2):
            mine = is_mine(g, half)

            @pl.when(mine)
            def _(half=half):
                pltpu.make_async_copy(zsend.at[g, half], zrecv.at[z], zr).start()

            @pl.when(jnp.logical_not(mine))
            def _(half=half):
                z_copy(g, half).start()

    attention(0)
    attention(1)
    attention(2)
    forward_hidden()
    finish(0)
    attention(3)
    finish(1)
    turn_hidden()
    finish(2)
    product(0)
    finish(3)
    product(1)
    product(2)
    y_sum(0)
    product(3)
    y_sum(1)
    y_sum(2)
    y_sum(3)

    wait_bytes(hall.at[1:4], hs.at[0])
    wait_bytes(hall.at[4:8], hs.at[1])
    for g in range(KV_HEADS):
        wait_bytes(kwin.at[g, 0], kvs.at[g])
        contribs(g).wait_send()
        wait_bytes(kall.at[g, 1:8], xs.at[g])
        wait_bytes(yrecv.at[g, 1:8], ys.at[g])
        for c in out_copies(g):
            c.wait()
        for half in range(2):
            @pl.when(jnp.logical_not(is_mine(g, half)))
            def _(half=half):
                z_copy(g, half).wait_send()

    wait_bytes(zrecv, zr)
    w = zrecv[0]
    for k in range(1, Z):
        w = w + zrecv[k]

    gpart[...] = mm(w, w, ((0,), (0,)), precision=HIGHEST).reshape(8, 16, HEAD_DIM)
    for k in (6, 7, 4, 5, 2, 3, 1):
        remote(gpart.at[lax.rem(cell + k, 8)], g1buf.at[k], g1s, g1r, cell_dev(k)).start()
    total = gpart[cell]
    wait_bytes(g1buf.at[1:8], g1r)
    for k in range(1, 8):
        total = total + g1buf[k]
    s1[...] = total
    for k in (4, 3, 5, 2, 6, 1, 7):
        remote(s1, g2buf.at[k], g2s, g2r, z_dev(k)).start()
    wait_bytes(g1buf.at[1:8], g1s)
    wait_bytes(g2buf.at[1:8], g2r)
    for k in range(1, 8):
        total = total + g2buf[k]
    gfull[cell] = total
    for k in (6, 7, 4, 5, 2, 3, 1):
        remote(gfull.at[cell], gfull.at[cell], g3s, g3r, cell_dev(k)).start()
    wait_bytes(g2buf.at[1:8], g2s)
    wait_bytes(g1buf.at[1:8], g3r)
    gram = gfull[...].reshape(HEAD_DIM, HEAD_DIM)

    ident = jnp.where(eye, 1.0, 0.0)
    norm = jnp.sqrt(jnp.sum(jnp.sum(gram * ident, axis=1, keepdims=True), axis=0, keepdims=True))
    inv = 1.0 / (norm + 1e-07)
    gram = gram * inv * inv

    def dot(a, b):
        return mm(a, b, ((1,), (0,)), precision=HIGHEST)

    run = None
    for it in range(NS_ITERS):
        poly = coeff_a * ident + coeff_b * gram + coeff_c * dot(gram, gram)
        run = poly if run is None else dot(run, poly)
        if it < NS_ITERS - 1:
            gram = dot(dot(poly, gram), poly)
    up_out[0] = dot(w * (inv * math.sqrt(D)), run)
    wait_bytes(g1buf.at[1:8], g3s)


def shards(hidden, queries, keys, values, out_grad, doc_ids):
    any_spec = pl.BlockSpec(memory_space=pl.ANY)
    vmem = pl.BlockSpec(memory_space=pltpu.VMEM)
    dma = pltpu.SemaphoreType.DMA
    heads = KV_HEADS
    return pl.pallas_call(
        kernel,
        out_shape=(
            jax.ShapeDtypeStruct((1, TOK, 2 * KV_W), BF16),
            jax.ShapeDtypeStruct((1, ROWS, HEAD_DIM), F32),
        ),
        in_specs=[any_spec] * 5 + [vmem],
        out_specs=(any_spec, vmem),
        scratch_shapes=[
            pltpu.VMEM((TOK, heads * HEADS_W), BF16),
            pltpu.VMEM((TOK, heads * HEADS_W), BF16),
            pltpu.VMEM((heads, 2, 2, TOK, HEAD_DIM), BF16),
            pltpu.VMEM((2 * TOK, TOK), F32),
            pltpu.VMEM((HEADS_W, HEAD_DIM), BF16),
            pltpu.VMEM((HEADS_W, HEAD_DIM), BF16),
            pltpu.VMEM((2 * TOK, HEADS_W), BF16),
            pltpu.VMEM((2 * TOK, HEADS_W), BF16),
            pltpu.VMEM((heads, 2, TOK, HEAD_DIM), F32),
            pltpu.VMEM((heads, 2, TOK, HEAD_DIM), F32),
            pltpu.VMEM((heads, 2, TOK, HEAD_DIM), F32),
            pltpu.VMEM((heads, 2, TOK, HEAD_DIM), BF16),
            pltpu.VMEM((8, TOK, QUARTER), BF16),
            pltpu.VMEM((QUARTER, 8 * TOK), BF16),
            pltpu.VMEM((heads, 8, TOK, HEAD_DIM), BF16),
            pltpu.VMEM((heads, Y, CHUNK, HEAD_DIM), F32),
            pltpu.VMEM((heads, Y, CHUNK, HEAD_DIM), BF16),
            pltpu.VMEM((heads, Y, CHUNK, HEAD_DIM), BF16),
            pltpu.VMEM((heads, 2, ROWS, HEAD_DIM), F32),
            pltpu.VMEM((Z, ROWS, HEAD_DIM), F32),
            pltpu.VMEM((8, 16, HEAD_DIM), F32),
            pltpu.VMEM((8, 16, HEAD_DIM), F32),
            pltpu.VMEM((16, HEAD_DIM), F32),
            pltpu.VMEM((8, 16, HEAD_DIM), F32),
            pltpu.VMEM((8, 16, HEAD_DIM), F32),
            dma((heads, 4)), dma,
            dma((heads,)), dma((heads,)),
            dma((2,)), dma((2,)),
            dma((heads,)), dma((heads,)),
            dma((heads,)), dma((heads,)),
            dma((heads,)), dma((heads,)),
            dma((heads, 2)), dma,
            dma, dma,
            dma, dma,
            dma, dma,
            dma((2 * heads,)),
        ],
        compiler_params=pltpu.CompilerParams(
            collective_id=0, has_side_effects=True, vmem_limit_bytes=56 * 1024 * 1024
        ),
        name="muon_kv_grads",
    )(hidden, queries, keys, values, out_grad, doc_ids)


def solution(mesh):
    placed = (P("fsdp", "ctx", None),) * 5 + (P("fsdp", None),)
    return jax.shard_map(
        shards,
        mesh=mesh,
        in_specs=placed,
        out_specs=(P("fsdp", "ctx", None), P("fsdp", "ctx", None)),
        check_vma=False,
    )
```

```python
import math

import jax
import jax.numpy as jnp
from jax import lax
from jax.experimental import pallas as pl
from jax.experimental.pallas import tpu as pltpu
from jax.sharding import PartitionSpec as P

D = 2560
KV_HEADS = 4
GROUP = 12
HEAD_DIM = 128
NS_ITERS = 5
TOK = 128
X, Y, Z, YL = 4, 8, 8, 4
QUARTER = D // X
CHUNK = QUARTER // Y
ROWS = CHUNK // 2
HEADS_W = GROUP * HEAD_DIM
KV_W = KV_HEADS * HEAD_DIM

coeff_a = 3.4445
coeff_b = -4.775
coeff_c = 2.0315

F32 = jnp.float32
BF16 = jnp.bfloat16
MESH = pl.DeviceIdType.MESH
HIGHEST = lax.Precision.HIGHEST


def device(x, yh, yl, z, core):
    return {"ctx": z * 8 + yl * 2 + core, "fsdp": yh * 4 + x}


def remote(src, dst, send, recv, to):
    return pltpu.make_async_remote_copy(
        src_ref=src, dst_ref=dst, send_sem=send, recv_sem=recv, device_id=to, device_id_type=MESH
    )


def mm(a, b, dims, **kw):
    return lax.dot_general(a, b, ((dims[0], dims[1]), ((), ())), preferred_element_type=F32, **kw)


def wait_bytes(ref, sem):
    pltpu.make_async_copy(ref, ref, sem).wait()


def kernel(
    hid, qs, ks, vs, og, docs, kv_out, up_out,
    q_v, g_v, kwin, bias, qst, gst, dsb, pbb, csend, cown, crecv, kvb, hall, ht, kall, w32, wlo,
    yrecv, zsend, zrecv, gpart, g1buf, s1, g2buf, gfull,
    word_y, word_z, loc, loh, kvs, kvr, hs, hr, cs, cr, xs, xr, ys, yr, zs, zr, g1s, g1r, g2s, g2r, g3s, g3r, outs,
):
    ctx, fsdp = lax.axis_index("ctx"), lax.axis_index("fsdp")
    z, yl, core = ctx // 8, lax.rem(ctx // 2, YL), lax.rem(ctx, 2)
    yh, x = fsdp // X, lax.rem(fsdp, X)
    y = yh * YL + yl
    cell = yl * 2 + core
    nxt, prv = lax.rem(ctx + 1, 64), lax.rem(ctx + 63, 64)

    def x_dev(dx, dc):
        return device(lax.rem(x + dx, X), yh, yl, z, lax.rem(core + dc, 2))

    def y_dev(k):
        to = lax.rem(y + k, Y)
        return device(x, to // YL, lax.rem(to, YL), z, core)

    def cell_dev(k):
        return {"ctx": z * 8 + lax.rem(cell + k, 8), "fsdp": fsdp}

    def z_dev(k):
        return {"ctx": lax.rem(z + k, Z) * 8 + cell, "fsdp": fsdp}

    def first_dev(g, k):
        return z_dev(k) if g % 2 else y_dev(k)

    def place(g):
        return z if g % 2 else y

    def owner(g, half):
        where = place(g)
        return device(g, core, lax.rem(where, YL), 2 * x + where // YL, half)

    def is_mine(g, half):
        where = place(g)
        here = jnp.logical_and(yl == lax.rem(where, YL), z == 2 * x + where // YL)
        return jnp.logical_and(jnp.logical_and(x == g, core == half), jnp.logical_and(core == yh, here))

    barrier = pltpu.get_barrier_semaphore()

    def greet(to):
        pl.semaphore_signal(barrier, inc=1, device_id=to, device_id_type=MESH)

    greet({"ctx": nxt, "fsdp": fsdp})
    greet({"ctx": prv, "fsdp": fsdp})
    for k in range(1, 8):
        greet(x_dev(k % 4, k // 4))
        greet(y_dev(k))
        greet(cell_dev(k))
        greet(z_dev(k))
    greeted = 2 + 4 * 7

    def loads(g):
        wide = slice(g * HEADS_W, (g + 1) * HEADS_W)
        lanes = slice(g * HEAD_DIM, (g + 1) * HEAD_DIM)
        return (
            pltpu.make_async_copy(qs.at[0, :, wide], q_v.at[:, wide], loc.at[g, 0]),
            pltpu.make_async_copy(og.at[0, :, wide], g_v.at[:, wide], loc.at[g, 1]),
            pltpu.make_async_copy(ks.at[0, :, lanes], kwin.at[g, 1, 0], loc.at[g, 2]),
            pltpu.make_async_copy(vs.at[0, :, lanes], kwin.at[g, 1, 1], loc.at[g, 3]),
        )

    def hidden_cols(which):
        return hid.at[0, :, pl.ds(pl.multiple_of(which * QUARTER, 128), QUARTER)]

    own_h = pltpu.make_async_copy(hidden_cols(x), hall.at[0], loh)
    for c in loads(0):
        c.start()

    eye = lax.broadcasted_iota(jnp.int32, (TOK, TOK), 0) == lax.broadcasted_iota(jnp.int32, (TOK, TOK), 1)
    own_row = docs[:, pl.ds(pl.multiple_of(ctx * TOK, TOK), TOK)].astype(F32)
    prv_row = docs[:, pl.ds(pl.multiple_of(prv * TOK, TOK), TOK)].astype(F32)
    prv_row = jnp.where(ctx == 0, -1.0, prv_row)

    def as_column(row):
        return jnp.sum(jnp.where(eye, jnp.broadcast_to(row, (TOK, TOK)), 0.0), axis=1, keepdims=True)

    earlier = lax.broadcasted_iota(jnp.int32, (TOK, TOK), 0) <= lax.broadcasted_iota(jnp.int32, (TOK, TOK), 1)
    bias[0:TOK, :] = jnp.where(as_column(prv_row) == own_row, 0.0, -1e30)
    bias[TOK:, :] = jnp.where(jnp.logical_and(as_column(own_row) == own_row, earlier), 0.0, -1e30)

    pl.semaphore_wait(barrier, greeted)

    def window(g):
        lanes = slice(g * HEAD_DIM, (g + 1) * HEAD_DIM)
        to = {"ctx": nxt, "fsdp": fsdp}
        return (
            remote(ks.at[0, :, lanes], kwin.at[g, 0, 0], kvs.at[g], kvr.at[g], to),
            remote(vs.at[0, :, lanes], kwin.at[g, 0, 1], kvs.at[g], kvr.at[g], to),
        )

    for g in range(KV_HEADS):
        for c in window(g):
            c.start()
    for dx in (2, 1, 3):
        remote(hidden_cols(lax.rem(x + dx, X)), hall.at[dx], hs.at[0], hr.at[0], x_dev(dx, 0)).start()
    remote(hidden_cols(x), hall.at[4], hs.at[1], hr.at[1], x_dev(0, 1)).start()
    for g in range(1, KV_HEADS):
        for c in loads(g):
            c.start()
    own_h.start()

    for k in range(1, 8):
        pl.semaphore_signal(word_y, inc=1, device_id=y_dev(k), device_id_type=MESH)

    def pass_word():
        pl.semaphore_wait(word_y, 7)
        for k in range(1, 8):
            pl.semaphore_signal(word_z, inc=1, device_id=z_dev(k), device_id_type=MESH)

    def forward_hidden():
        wait_bytes(hall.at[1:4], hr.at[0])
        for dx in range(1, X):
            remote(hall.at[dx], hall.at[4 + dx], hs.at[1], hr.at[1], x_dev(0, 1)).start()

    def turn_hidden():
        own_h.wait()
        wait_bytes(hall.at[4:8], hr.at[1])
        for k in range(8):
            ht[:, k * TOK:(k + 1) * TOK] = hall[k].T

    scale = 1.0 / math.sqrt(HEAD_DIM)
    scale2 = scale * math.log2(math.e)

    def contribs(g):
        return remote(csend.at[g], crecv.at[g], cs.at[g], cr.at[g], {"ctx": prv, "fsdp": fsdp})

    def attention(g):
        for c in loads(g):
            c.wait()
        wait_bytes(kwin.at[g, 0], kvr.at[g])
        kw = jnp.concatenate([kwin[g, 0, 0], kwin[g, 1, 0]], axis=0)
        vw = jnp.concatenate([kwin[g, 0, 1], kwin[g, 1, 1]], axis=0)
        both = jnp.concatenate([bias[...], bias[...]], axis=1)
        for i in range(GROUP // 2):
            at = [slice((g * GROUP + 2 * i + j) * HEAD_DIM, (g * GROUP + 2 * i + j + 1) * HEAD_DIM) for j in range(2)]
            q2 = jnp.concatenate([q_v[:, at[0]], q_v[:, at[1]]], axis=0)
            g2 = jnp.concatenate([g_v[:, at[0]], g_v[:, at[1]]], axis=0)
            s = mm(kw, q2, ((1,), (1,))) * scale2 + both
            dp = mm(vw, g2, ((1,), (1,)))
            e = jnp.exp2(s - jnp.max(s, axis=0, keepdims=True))
            inv = 1.0 / jnp.sum(e, axis=0, keepdims=True)
            p = e * inv
            delta = jnp.sum(p * dp, axis=0, keepdims=True)
            cols = slice(2 * i * HEAD_DIM, 2 * (i + 1) * HEAD_DIM)
            dsb[:, cols] = (p * (dp - delta)).astype(BF16)
            pbb[:, cols] = p.astype(BF16)
            qst[cols, :] = q2
            gst[cols, :] = g2
        csend[g, 0] = mm(dsb[0:TOK, :], qst[...], ((1,), (0,))) * scale
        csend[g, 1] = mm(pbb[0:TOK, :], gst[...], ((1,), (0,)))
        contribs(g).start()
        cown[g, 0] = mm(dsb[TOK:, :], qst[...], ((1,), (0,))) * scale
        cown[g, 1] = mm(pbb[TOK:, :], gst[...], ((1,), (0,)))

    def out_copies(g):
        return [
            pltpu.make_async_copy(
                kvb.at[g, j], kv_out.at[0, :, j * KV_W + g * HEAD_DIM:j * KV_W + (g + 1) * HEAD_DIM], outs.at[2 * g + j]
            )
            for j in range(2)
        ]

    def finish(g):
        contribs(g).wait_recv()
        kvb[g] = (crecv[g] + cown[g]).astype(BF16)
        for k in (2, 6, 1, 3, 5, 7, 4):
            remote(
                kvb.at[g, lax.rem(core + k // 4, 2)], kall.at[g, k], xs.at[g], xr.at[g], x_dev(k % 4, k // 4)
            ).start()
        kall[g, 0] = kvb[g, core]
        for c in out_copies(g):
            c.start()

    def product(g):
        wait_bytes(kall.at[g, 1:8], xr.at[g])
        w = mm(ht[...], kall[g].reshape(8 * TOK, HEAD_DIM), ((1,), (0,))).reshape(Y, CHUNK, HEAD_DIM)
        wlo[g] = w.astype(BF16)
        for k in (4, 3, 5, 2, 6, 1, 7):
            remote(wlo.at[g, lax.rem(place(g) + k, Y)], yrecv.at[g, k], ys.at[g], yr.at[g], first_dev(g, k)).start()
        w32[g] = w

    def z_copy(g, half):
        return remote(zsend.at[g, half], zrecv.at[place(g + 1)], zs.at[g, half], zr, owner(g, half))

    def y_sum(g):
        wait_bytes(yrecv.at[g, 1:8], yr.at[g])
        total = w32[g, place(g)]
        for k in range(1, Y):
            total = total + yrecv[g, k].astype(F32)
        zsend[g] = total.reshape(2, ROWS, HEAD_DIM)
        for half in range(2):
            mine = is_mine(g, half)

            @pl.when(mine)
            def _(half=half):
                pltpu.make_async_copy(zsend.at[g, half], zrecv.at[place(g + 1)], zr).start()

            @pl.when(jnp.logical_not(mine))
            def _(half=half):
                z_copy(g, half).start()

    attention(0)
    attention(1)
    attention(2)
    finish(0)
    attention(3)
    finish(1)
    forward_hidden()
    pass_word()
    finish(2)
    turn_hidden()
    product(0)
    finish(3)
    product(1)
    product(2)
    pl.semaphore_wait(word_z, 7)
    y_sum(0)
    product(3)
    y_sum(1)
    y_sum(2)
    y_sum(3)

    wait_bytes(hall.at[1:4], hs.at[0])
    wait_bytes(hall.at[4:8], hs.at[1])
    for g in range(KV_HEADS):
        wait_bytes(kwin.at[g, 0], kvs.at[g])
        contribs(g).wait_send()
        wait_bytes(kall.at[g, 1:8], xs.at[g])
        wait_bytes(yrecv.at[g, 1:8], ys.at[g])
        for c in out_copies(g):
            c.wait()
        for half in range(2):
            @pl.when(jnp.logical_not(is_mine(g, half)))
            def _(half=half):
                z_copy(g, half).wait_send()

    wait_bytes(zrecv, zr)
    w = zrecv[0]
    for k in range(1, Z):
        w = w + zrecv[k]

    gpart[...] = mm(w, w, ((0,), (0,)), precision=HIGHEST).reshape(8, 16, HEAD_DIM)
    for k in (6, 7, 4, 5, 2, 3, 1):
        remote(gpart.at[lax.rem(cell + k, 8)], g1buf.at[k], g1s, g1r, cell_dev(k)).start()
    total = gpart[cell]
    wait_bytes(g1buf.at[1:8], g1r)
    for k in range(1, 8):
        total = total + g1buf[k]
    s1[...] = total
    for k in (4, 3, 5, 2, 6, 1, 7):
        remote(s1, g2buf.at[k], g2s, g2r, z_dev(k)).start()
    wait_bytes(g1buf.at[1:8], g1s)
    wait_bytes(g2buf.at[1:8], g2r)
    for k in range(1, 8):
        total = total + g2buf[k]
    gfull[cell] = total
    for k in (6, 7, 4, 5, 2, 3, 1):
        remote(gfull.at[cell], gfull.at[cell], g3s, g3r, cell_dev(k)).start()
    wait_bytes(g2buf.at[1:8], g2s)
    wait_bytes(g1buf.at[1:8], g3r)
    gram = gfull[...].reshape(HEAD_DIM, HEAD_DIM)

    ident = jnp.where(eye, 1.0, 0.0)
    norm = jnp.sqrt(jnp.sum(jnp.sum(gram * ident, axis=1, keepdims=True), axis=0, keepdims=True))
    inv = 1.0 / (norm + 1e-07)
    gram = gram * inv * inv

    def dot(a, b):
        return mm(a, b, ((1,), (0,)), precision=HIGHEST)

    run = None
    for it in range(NS_ITERS):
        poly = coeff_a * ident + coeff_b * gram + coeff_c * dot(gram, gram)
        run = poly if run is None else dot(run, poly)
        if it < NS_ITERS - 1:
            gram = dot(dot(poly, gram), poly)
    up_out[0] = dot(w * (inv * math.sqrt(D)), run)
    wait_bytes(g1buf.at[1:8], g3s)


def write_results(kv, up, kv_out, up_out, kv_v, up_v, sems):
    pairs = [(up.at[0], up_v, up_out.at[0], sems.at[4])]
    for i in range(4):
        rows = slice(i * 32, (i + 1) * 32)
        pairs.append((kv.at[0, rows], kv_v.at[rows], kv_out.at[0, rows], sems.at[i]))
    for src, mid, _, sem in pairs:
        pltpu.make_async_copy(src, mid, sem).start()
    for src, mid, dst, sem in pairs:
        pltpu.make_async_copy(src, mid, sem).wait()
        pltpu.make_async_copy(mid, dst, sem).start()
    for _, mid, dst, sem in pairs:
        pltpu.make_async_copy(mid, dst, sem).wait()


def shards(hidden, queries, keys, values, out_grad, doc_ids):
    any_spec = pl.BlockSpec(memory_space=pl.ANY)
    vmem = pl.BlockSpec(memory_space=pltpu.VMEM)
    dma = pltpu.SemaphoreType.DMA
    heads = KV_HEADS
    out_shape = (
        jax.ShapeDtypeStruct((1, TOK, 2 * KV_W), BF16),
        jax.ShapeDtypeStruct((1, ROWS, HEAD_DIM), F32),
    )
    results = pl.pallas_call(
        kernel,
        out_shape=out_shape,
        in_specs=[any_spec] * 5 + [vmem],
        out_specs=(any_spec, vmem),
        scratch_shapes=[
            pltpu.VMEM((TOK, heads * HEADS_W), BF16),
            pltpu.VMEM((TOK, heads * HEADS_W), BF16),
            pltpu.VMEM((heads, 2, 2, TOK, HEAD_DIM), BF16),
            pltpu.VMEM((2 * TOK, TOK), F32),
            pltpu.VMEM((HEADS_W, HEAD_DIM), BF16),
            pltpu.VMEM((HEADS_W, HEAD_DIM), BF16),
            pltpu.VMEM((2 * TOK, HEADS_W), BF16),
            pltpu.VMEM((2 * TOK, HEADS_W), BF16),
            pltpu.VMEM((heads, 2, TOK, HEAD_DIM), F32),
            pltpu.VMEM((heads, 2, TOK, HEAD_DIM), F32),
            pltpu.VMEM((heads, 2, TOK, HEAD_DIM), F32),
            pltpu.VMEM((heads, 2, TOK, HEAD_DIM), BF16),
            pltpu.VMEM((8, TOK, QUARTER), BF16),
            pltpu.VMEM((QUARTER, 8 * TOK), BF16),
            pltpu.VMEM((heads, 8, TOK, HEAD_DIM), BF16),
            pltpu.VMEM((heads, Y, CHUNK, HEAD_DIM), F32),
            pltpu.VMEM((heads, Y, CHUNK, HEAD_DIM), BF16),
            pltpu.VMEM((heads, Y, CHUNK, HEAD_DIM), BF16),
            pltpu.VMEM((heads, 2, ROWS, HEAD_DIM), F32),
            pltpu.VMEM((Z, ROWS, HEAD_DIM), F32),
            pltpu.VMEM((8, 16, HEAD_DIM), F32),
            pltpu.VMEM((8, 16, HEAD_DIM), F32),
            pltpu.VMEM((16, HEAD_DIM), F32),
            pltpu.VMEM((8, 16, HEAD_DIM), F32),
            pltpu.VMEM((8, 16, HEAD_DIM), F32),
            pltpu.SemaphoreType.REGULAR, pltpu.SemaphoreType.REGULAR,
            dma((heads, 4)), dma,
            dma((heads,)), dma((heads,)),
            dma((2,)), dma((2,)),
            dma((heads,)), dma((heads,)),
            dma((heads,)), dma((heads,)),
            dma((heads,)), dma((heads,)),
            dma((heads, 2)), dma,
            dma, dma,
            dma, dma,
            dma, dma,
            dma((2 * heads,)),
        ],
        compiler_params=pltpu.CompilerParams(
            collective_id=0, has_side_effects=True, vmem_limit_bytes=56 * 1024 * 1024
        ),
        name="muon_kv_grads",
    )(hidden, queries, keys, values, out_grad, doc_ids)
    return pl.pallas_call(
        write_results,
        out_shape=out_shape,
        in_specs=[any_spec] * 2,
        out_specs=(any_spec, any_spec),
        scratch_shapes=[
            pltpu.VMEM((TOK, 2 * KV_W), BF16),
            pltpu.VMEM((ROWS, HEAD_DIM), F32),
            dma((5,)),
        ],
        compiler_params=pltpu.CompilerParams(vmem_limit_bytes=56 * 1024 * 1024),
        name="write_results",
    )(*results)


def solution(mesh):
    placed = (P("fsdp", "ctx", None),) * 5 + (P("fsdp", None),)
    return jax.shard_map(
        shards,
        mesh=mesh,
        in_specs=placed,
        out_specs=(P("fsdp", "ctx", None), P("fsdp", "ctx", None)),
        check_vma=False,
    )
```

```python
import math

import jax
import jax.numpy as jnp
from jax import lax
from jax.experimental import pallas as pl
from jax.experimental.pallas import tpu as pltpu
from jax.sharding import PartitionSpec as P

D = 2560
KV_HEADS = 4
GROUP = 12
HEAD_DIM = 128
NS_ITERS = 5
TOK = 128
X, Y, Z, YL = 4, 8, 8, 4
QUARTER = D // X
CHUNK = QUARTER // Y
ROWS = CHUNK // 2
HEADS_W = GROUP * HEAD_DIM
KV_W = KV_HEADS * HEAD_DIM
Z_FIRST = (1,)

coeff_a = 3.4445
coeff_b = -4.775
coeff_c = 2.0315

F32 = jnp.float32
BF16 = jnp.bfloat16
MESH = pl.DeviceIdType.MESH
HIGHEST = lax.Precision.HIGHEST


def device(x, yh, yl, z, core):
    return {"ctx": z * 8 + yl * 2 + core, "fsdp": yh * 4 + x}


def remote(src, dst, send, recv, to):
    return pltpu.make_async_remote_copy(
        src_ref=src, dst_ref=dst, send_sem=send, recv_sem=recv, device_id=to, device_id_type=MESH
    )


def mm(a, b, dims, **kw):
    return lax.dot_general(a, b, ((dims[0], dims[1]), ((), ())), preferred_element_type=F32, **kw)


def wait_bytes(ref, sem):
    pltpu.make_async_copy(ref, ref, sem).wait()


def kernel(
    hid, qs, ks, vs, og, docs, kv_out, up_out,
    q_v, g_v, kwin, bias, qst, gst, dsb, pbb, csend, cown, crecv, kvb, hall, ht, kall, w32, wlo,
    yrecv, zsend, zrecv, gpart, g1buf, s1, g2buf, gfull,
    word_y, word_z, loc, loh, kvs, kvr, hs, hr, cs, cr, xs, xr, ys, yr, zs, zr, g1s, g1r, g2s, g2r, g3s, g3r, outs,
):
    ctx, fsdp = lax.axis_index("ctx"), lax.axis_index("fsdp")
    z, yl, core = ctx // 8, lax.rem(ctx // 2, YL), lax.rem(ctx, 2)
    yh, x = fsdp // X, lax.rem(fsdp, X)
    y = yh * YL + yl
    cell = yl * 2 + core
    nxt, prv = lax.rem(ctx + 1, 64), lax.rem(ctx + 63, 64)

    def x_dev(dx, dc):
        return device(lax.rem(x + dx, X), yh, yl, z, lax.rem(core + dc, 2))

    def y_dev(k):
        to = lax.rem(y + k, Y)
        return device(x, to // YL, lax.rem(to, YL), z, core)

    def cell_dev(k):
        return {"ctx": z * 8 + lax.rem(cell + k, 8), "fsdp": fsdp}

    def z_dev(k):
        return {"ctx": lax.rem(z + k, Z) * 8 + cell, "fsdp": fsdp}

    def first_dev(g, k):
        return z_dev(k) if g in Z_FIRST else y_dev(k)

    def place(g):
        return z if g in Z_FIRST else y

    def owner(g, half):
        where = place(g)
        return device(g, core, lax.rem(where, YL), 2 * x + where // YL, half)

    def is_mine(g, half):
        where = place(g)
        here = jnp.logical_and(yl == lax.rem(where, YL), z == 2 * x + where // YL)
        return jnp.logical_and(jnp.logical_and(x == g, core == half), jnp.logical_and(core == yh, here))

    def owner_slot(g):
        return y if g in Z_FIRST else z

    barrier = pltpu.get_barrier_semaphore()

    def greet(to):
        pl.semaphore_signal(barrier, inc=1, device_id=to, device_id_type=MESH)

    greet({"ctx": nxt, "fsdp": fsdp})
    greet({"ctx": prv, "fsdp": fsdp})
    for k in range(1, 8):
        greet(x_dev(k % 4, k // 4))
        greet(y_dev(k))
        greet(cell_dev(k))
        greet(z_dev(k))
    greeted = 2 + 4 * 7

    def loads(g):
        wide = slice(g * HEADS_W, (g + 1) * HEADS_W)
        lanes = slice(g * HEAD_DIM, (g + 1) * HEAD_DIM)
        return (
            pltpu.make_async_copy(qs.at[0, :, wide], q_v.at[:, wide], loc.at[g, 0]),
            pltpu.make_async_copy(og.at[0, :, wide], g_v.at[:, wide], loc.at[g, 1]),
            pltpu.make_async_copy(ks.at[0, :, lanes], kwin.at[g, 1, 0], loc.at[g, 2]),
            pltpu.make_async_copy(vs.at[0, :, lanes], kwin.at[g, 1, 1], loc.at[g, 3]),
        )

    def hidden_cols(which):
        return hid.at[0, :, pl.ds(pl.multiple_of(which * QUARTER, 128), QUARTER)]

    own_h = pltpu.make_async_copy(hidden_cols(x), hall.at[0], loh)
    for c in loads(0):
        c.start()

    eye = lax.broadcasted_iota(jnp.int32, (TOK, TOK), 0) == lax.broadcasted_iota(jnp.int32, (TOK, TOK), 1)
    own_row = docs[:, pl.ds(pl.multiple_of(ctx * TOK, TOK), TOK)].astype(F32)
    prv_row = docs[:, pl.ds(pl.multiple_of(prv * TOK, TOK), TOK)].astype(F32)
    prv_row = jnp.where(ctx == 0, -1.0, prv_row)

    def as_column(row):
        return jnp.sum(jnp.where(eye, jnp.broadcast_to(row, (TOK, TOK)), 0.0), axis=1, keepdims=True)

    earlier = lax.broadcasted_iota(jnp.int32, (TOK, TOK), 0) <= lax.broadcasted_iota(jnp.int32, (TOK, TOK), 1)
    bias[0:TOK, :] = jnp.where(as_column(prv_row) == own_row, 0.0, -1e30)
    bias[TOK:, :] = jnp.where(jnp.logical_and(as_column(own_row) == own_row, earlier), 0.0, -1e30)

    pl.semaphore_wait(barrier, greeted)

    def window(g):
        lanes = slice(g * HEAD_DIM, (g + 1) * HEAD_DIM)
        to = {"ctx": nxt, "fsdp": fsdp}
        return (
            remote(ks.at[0, :, lanes], kwin.at[g, 0, 0], kvs.at[g], kvr.at[g], to),
            remote(vs.at[0, :, lanes], kwin.at[g, 0, 1], kvs.at[g], kvr.at[g], to),
        )

    for g in range(KV_HEADS):
        for c in window(g):
            c.start()
    for dx in (2, 1, 3):
        remote(hidden_cols(lax.rem(x + dx, X)), hall.at[dx], hs.at[0], hr.at[0], x_dev(dx, 0)).start()
    remote(hidden_cols(x), hall.at[4], hs.at[1], hr.at[1], x_dev(0, 1)).start()
    for g in range(1, KV_HEADS):
        for c in loads(g):
            c.start()
    own_h.start()

    for k in range(1, 8):
        pl.semaphore_signal(word_y, inc=1, device_id=y_dev(k), device_id_type=MESH)

    def pass_word():
        pl.semaphore_wait(word_y, 7)
        for k in range(1, 8):
            pl.semaphore_signal(word_z, inc=1, device_id=z_dev(k), device_id_type=MESH)

    def forward_hidden():
        wait_bytes(hall.at[1:4], hr.at[0])
        for dx in range(1, X):
            remote(hall.at[dx], hall.at[4 + dx], hs.at[1], hr.at[1], x_dev(0, 1)).start()

    def turn_hidden():
        own_h.wait()
        wait_bytes(hall.at[4:8], hr.at[1])
        for k in range(8):
            ht[:, k * TOK:(k + 1) * TOK] = hall[k].T

    scale = 1.0 / math.sqrt(HEAD_DIM)
    scale2 = scale * math.log2(math.e)

    def contribs(g):
        return remote(csend.at[g], crecv.at[g], cs.at[g], cr.at[g], {"ctx": prv, "fsdp": fsdp})

    def attention(g):
        for c in loads(g):
            c.wait()
        wait_bytes(kwin.at[g, 0], kvr.at[g])
        kw = jnp.concatenate([kwin[g, 0, 0], kwin[g, 1, 0]], axis=0)
        vw = jnp.concatenate([kwin[g, 0, 1], kwin[g, 1, 1]], axis=0)
        both = jnp.concatenate([bias[...], bias[...]], axis=1)
        for i in range(GROUP // 2):
            at = [slice((g * GROUP + 2 * i + j) * HEAD_DIM, (g * GROUP + 2 * i + j + 1) * HEAD_DIM) for j in range(2)]
            q2 = jnp.concatenate([q_v[:, at[0]], q_v[:, at[1]]], axis=0)
            g2 = jnp.concatenate([g_v[:, at[0]], g_v[:, at[1]]], axis=0)
            s = mm(kw, q2, ((1,), (1,))) * scale2 + both
            dp = mm(vw, g2, ((1,), (1,)))
            e = jnp.exp2(s - jnp.max(s, axis=0, keepdims=True))
            inv = 1.0 / jnp.sum(e, axis=0, keepdims=True)
            p = e * inv
            delta = jnp.sum(p * dp, axis=0, keepdims=True)
            cols = slice(2 * i * HEAD_DIM, 2 * (i + 1) * HEAD_DIM)
            dsb[:, cols] = (p * (dp - delta)).astype(BF16)
            pbb[:, cols] = p.astype(BF16)
            qst[cols, :] = q2
            gst[cols, :] = g2
        csend[g, 0] = mm(dsb[0:TOK, :], qst[...], ((1,), (0,))) * scale
        csend[g, 1] = mm(pbb[0:TOK, :], gst[...], ((1,), (0,)))
        contribs(g).start()
        cown[g, 0] = mm(dsb[TOK:, :], qst[...], ((1,), (0,))) * scale
        cown[g, 1] = mm(pbb[TOK:, :], gst[...], ((1,), (0,)))

    def out_copies(g):
        return [
            pltpu.make_async_copy(
                kvb.at[g, j], kv_out.at[0, :, j * KV_W + g * HEAD_DIM:j * KV_W + (g + 1) * HEAD_DIM], outs.at[2 * g + j]
            )
            for j in range(2)
        ]

    def finish(g):
        contribs(g).wait_recv()
        kvb[g] = (crecv[g] + cown[g]).astype(BF16)
        for k in (2, 6, 1, 3, 5, 7, 4):
            remote(
                kvb.at[g, lax.rem(core + k // 4, 2)], kall.at[g, k], xs.at[g], xr.at[g], x_dev(k % 4, k // 4)
            ).start()
        kall[g, 0] = kvb[g, core]
        for c in out_copies(g):
            c.start()

    def product(g):
        wait_bytes(kall.at[g, 1:8], xr.at[g])
        w = mm(ht[...], kall[g].reshape(8 * TOK, HEAD_DIM), ((1,), (0,))).reshape(Y, CHUNK, HEAD_DIM)
        wlo[g] = w.astype(BF16)
        for k in (4, 3, 5, 2, 6, 1, 7):
            remote(wlo.at[g, lax.rem(place(g) + k, Y)], yrecv.at[g, k], ys.at[g], yr.at[g], first_dev(g, k)).start()
        w32[g] = w

    def z_copy(g, half):
        return remote(zsend.at[g, half], zrecv.at[owner_slot(g)], zs.at[g, half], zr, owner(g, half))

    def y_sum(g):
        wait_bytes(yrecv.at[g, 1:8], yr.at[g])
        total = w32[g, place(g)]
        for k in range(1, Y):
            total = total + yrecv[g, k].astype(F32)
        zsend[g] = total.reshape(2, ROWS, HEAD_DIM)
        for half in range(2):
            mine = is_mine(g, half)

            @pl.when(mine)
            def _(half=half):
                pltpu.make_async_copy(zsend.at[g, half], zrecv.at[owner_slot(g)], zr).start()

            @pl.when(jnp.logical_not(mine))
            def _(half=half):
                z_copy(g, half).start()

    attention(0)
    attention(1)
    finish(0)
    attention(2)
    finish(1)
    forward_hidden()
    attention(3)
    finish(2)
    turn_hidden()
    pass_word()
    product(0)
    finish(3)
    product(1)
    product(2)
    product(3)
    pl.semaphore_wait(word_z, 7)
    for g in range(KV_HEADS):
        y_sum(g)

    wait_bytes(hall.at[1:4], hs.at[0])
    wait_bytes(hall.at[4:8], hs.at[1])
    for g in range(KV_HEADS):
        wait_bytes(kwin.at[g, 0], kvs.at[g])
        contribs(g).wait_send()
        wait_bytes(kall.at[g, 1:8], xs.at[g])
        wait_bytes(yrecv.at[g, 1:8], ys.at[g])
        for c in out_copies(g):
            c.wait()
        for half in range(2):
            @pl.when(jnp.logical_not(is_mine(g, half)))
            def _(half=half):
                z_copy(g, half).wait_send()

    wait_bytes(zrecv, zr)
    w = zrecv[0]
    for k in range(1, Z):
        w = w + zrecv[k]

    gpart[...] = mm(w, w, ((0,), (0,)), precision=HIGHEST).reshape(8, 16, HEAD_DIM)
    for k in (6, 7, 4, 5, 2, 3, 1):
        remote(gpart.at[lax.rem(cell + k, 8)], g1buf.at[k], g1s, g1r, cell_dev(k)).start()
    total = gpart[cell]
    wait_bytes(g1buf.at[1:8], g1r)
    for k in range(1, 8):
        total = total + g1buf[k]
    s1[...] = total
    for k in (4, 3, 5, 2, 6, 1, 7):
        remote(s1, g2buf.at[k], g2s, g2r, z_dev(k)).start()
    wait_bytes(g1buf.at[1:8], g1s)
    wait_bytes(g2buf.at[1:8], g2r)
    for k in range(1, 8):
        total = total + g2buf[k]
    gfull[cell] = total
    for k in (6, 7, 4, 5, 2, 3, 1):
        remote(gfull.at[cell], gfull.at[cell], g3s, g3r, cell_dev(k)).start()
    wait_bytes(g2buf.at[1:8], g2s)
    wait_bytes(g1buf.at[1:8], g3r)
    gram = gfull[...].reshape(HEAD_DIM, HEAD_DIM)

    ident = jnp.where(eye, 1.0, 0.0)
    norm = jnp.sqrt(jnp.sum(jnp.sum(gram * ident, axis=1, keepdims=True), axis=0, keepdims=True))
    inv = 1.0 / (norm + 1e-07)
    gram = gram * inv * inv

    def parts(v):
        high = v.astype(BF16)
        rest = v - high.astype(F32)
        mid = rest.astype(BF16)
        return high, mid, (rest - mid.astype(F32)).astype(BF16)

    def left(p):
        return jnp.concatenate([p[2], p[0], p[1], p[1], p[0], p[0]], axis=1)

    def right(p):
        return jnp.concatenate([p[0], p[2], p[1], p[0], p[1], p[0]], axis=0)

    def dot(a, b):
        return mm(a, b, ((1,), (0,)))

    state = w * inv
    for it in range(NS_ITERS):
        gram_parts = parts(gram)
        gram_right = right(gram_parts)
        poly = coeff_a * ident + coeff_b * gram + coeff_c * dot(left(gram_parts), gram_right)
        poly_parts = parts(poly)
        poly_right = right(poly_parts)
        if it < NS_ITERS - 1:
            gram = dot(left(parts(dot(left(poly_parts), gram_right))), poly_right)
        state = dot(left(parts(state)), poly_right)
    up_out[0] = math.sqrt(D) * state
    wait_bytes(g1buf.at[1:8], g3s)


def write_results(kv, up, kv_out, up_out, kv_v, up_v, sems):
    pairs = [(up.at[0], up_v, up_out.at[0], sems.at[4])]
    for i in range(4):
        rows = slice(i * 32, (i + 1) * 32)
        pairs.append((kv.at[0, rows], kv_v.at[rows], kv_out.at[0, rows], sems.at[i]))
    for src, mid, _, sem in pairs:
        pltpu.make_async_copy(src, mid, sem).start()
    for src, mid, dst, sem in pairs:
        pltpu.make_async_copy(src, mid, sem).wait()
        pltpu.make_async_copy(mid, dst, sem).start()
    for _, mid, dst, sem in pairs:
        pltpu.make_async_copy(mid, dst, sem).wait()


def shards(hidden, queries, keys, values, out_grad, doc_ids):
    any_spec = pl.BlockSpec(memory_space=pl.ANY)
    vmem = pl.BlockSpec(memory_space=pltpu.VMEM)
    dma = pltpu.SemaphoreType.DMA
    heads = KV_HEADS
    out_shape = (
        jax.ShapeDtypeStruct((1, TOK, 2 * KV_W), BF16),
        jax.ShapeDtypeStruct((1, ROWS, HEAD_DIM), F32),
    )
    results = pl.pallas_call(
        kernel,
        out_shape=out_shape,
        in_specs=[any_spec] * 5 + [vmem],
        out_specs=(any_spec, vmem),
        scratch_shapes=[
            pltpu.VMEM((TOK, heads * HEADS_W), BF16),
            pltpu.VMEM((TOK, heads * HEADS_W), BF16),
            pltpu.VMEM((heads, 2, 2, TOK, HEAD_DIM), BF16),
            pltpu.VMEM((2 * TOK, TOK), F32),
            pltpu.VMEM((HEADS_W, HEAD_DIM), BF16),
            pltpu.VMEM((HEADS_W, HEAD_DIM), BF16),
            pltpu.VMEM((2 * TOK, HEADS_W), BF16),
            pltpu.VMEM((2 * TOK, HEADS_W), BF16),
            pltpu.VMEM((heads, 2, TOK, HEAD_DIM), F32),
            pltpu.VMEM((heads, 2, TOK, HEAD_DIM), F32),
            pltpu.VMEM((heads, 2, TOK, HEAD_DIM), F32),
            pltpu.VMEM((heads, 2, TOK, HEAD_DIM), BF16),
            pltpu.VMEM((8, TOK, QUARTER), BF16),
            pltpu.VMEM((QUARTER, 8 * TOK), BF16),
            pltpu.VMEM((heads, 8, TOK, HEAD_DIM), BF16),
            pltpu.VMEM((heads, Y, CHUNK, HEAD_DIM), F32),
            pltpu.VMEM((heads, Y, CHUNK, HEAD_DIM), BF16),
            pltpu.VMEM((heads, Y, CHUNK, HEAD_DIM), BF16),
            pltpu.VMEM((heads, 2, ROWS, HEAD_DIM), F32),
            pltpu.VMEM((Z, ROWS, HEAD_DIM), F32),
            pltpu.VMEM((8, 16, HEAD_DIM), F32),
            pltpu.VMEM((8, 16, HEAD_DIM), F32),
            pltpu.VMEM((16, HEAD_DIM), F32),
            pltpu.VMEM((8, 16, HEAD_DIM), F32),
            pltpu.VMEM((8, 16, HEAD_DIM), F32),
            pltpu.SemaphoreType.REGULAR, pltpu.SemaphoreType.REGULAR,
            dma((heads, 4)), dma,
            dma((heads,)), dma((heads,)),
            dma((2,)), dma((2,)),
            dma((heads,)), dma((heads,)),
            dma((heads,)), dma((heads,)),
            dma((heads,)), dma((heads,)),
            dma((heads, 2)), dma,
            dma, dma,
            dma, dma,
            dma, dma,
            dma((2 * heads,)),
        ],
        compiler_params=pltpu.CompilerParams(
            collective_id=0, has_side_effects=True, vmem_limit_bytes=56 * 1024 * 1024
        ),
        name="muon_kv_grads",
    )(hidden, queries, keys, values, out_grad, doc_ids)
    return pl.pallas_call(
        write_results,
        out_shape=out_shape,
        in_specs=[any_spec] * 2,
        out_specs=(any_spec, any_spec),
        scratch_shapes=[
            pltpu.VMEM((TOK, 2 * KV_W), BF16),
            pltpu.VMEM((ROWS, HEAD_DIM), F32),
            dma((5,)),
        ],
        compiler_params=pltpu.CompilerParams(vmem_limit_bytes=56 * 1024 * 1024),
        name="write_results",
    )(*results)


def solution(mesh):
    placed = (P("fsdp", "ctx", None),) * 5 + (P("fsdp", None),)
    return jax.shard_map(
        shards,
        mesh=mesh,
        in_specs=placed,
        out_specs=(P("fsdp", "ctx", None), P("fsdp", "ctx", None)),
        check_vma=False,
    )
```

```python
import math

import jax
import jax.numpy as jnp
from jax import lax
from jax.experimental import pallas as pl
from jax.experimental.pallas import tpu as pltpu
from jax.sharding import PartitionSpec as P

D = 2560
KV_HEADS = 4
GROUP = 12
HEAD_DIM = 128
NS_ITERS = 5
TOK = 128
X, Y, Z, YL = 4, 8, 8, 4
QUARTER = D // X
CHUNK = QUARTER // Y
ROWS = CHUNK // 2
HEADS_W = GROUP * HEAD_DIM
KV_W = KV_HEADS * HEAD_DIM
Z_FIRST = (1,)

coeff_a = 3.4445
coeff_b = -4.775
coeff_c = 2.0315

F32 = jnp.float32
BF16 = jnp.bfloat16
MESH = pl.DeviceIdType.MESH
HIGHEST = lax.Precision.HIGHEST


def device(x, yh, yl, z, core):
    return {"ctx": z * 8 + yl * 2 + core, "fsdp": yh * 4 + x}


def remote(src, dst, send, recv, to):
    return pltpu.make_async_remote_copy(
        src_ref=src, dst_ref=dst, send_sem=send, recv_sem=recv, device_id=to, device_id_type=MESH
    )


def mm(a, b, dims, **kw):
    return lax.dot_general(a, b, ((dims[0], dims[1]), ((), ())), preferred_element_type=F32, **kw)


def wait_bytes(ref, sem):
    pltpu.make_async_copy(ref, ref, sem).wait()


def kernel(
    hid, qs, ks, vs, og, docs, kv_out, up_out,
    q_v, g_v, kwin, bias, qst, gst, dsb, pbb, csend, cown, crecv, kvb, hall, ht, kall, w32, wlo,
    yrecv, zsend, zrecv, gpart, g1buf, s1, g2buf, gfull,
    word_y, word_z, loc, loh, kvs, kvr, hs, hr, cs, cr, xs, xr, ys, yr, zs, zr, g1s, g1r, g2s, g2r, g3s, g3r, outs,
):
    ctx, fsdp = lax.axis_index("ctx"), lax.axis_index("fsdp")
    z, yl, core = ctx // 8, lax.rem(ctx // 2, YL), lax.rem(ctx, 2)
    yh, x = fsdp // X, lax.rem(fsdp, X)
    y = yh * YL + yl
    cell = yl * 2 + core
    nxt, prv = lax.rem(ctx + 1, 64), lax.rem(ctx + 63, 64)

    def x_dev(dx, dc):
        return device(lax.rem(x + dx, X), yh, yl, z, lax.rem(core + dc, 2))

    def y_dev(k):
        to = lax.rem(y + k, Y)
        return device(x, to // YL, lax.rem(to, YL), z, core)

    def cell_dev(k):
        return {"ctx": z * 8 + lax.rem(cell + k, 8), "fsdp": fsdp}

    def z_dev(k):
        return {"ctx": lax.rem(z + k, Z) * 8 + cell, "fsdp": fsdp}

    def first_dev(g, k):
        return z_dev(k) if g in Z_FIRST else y_dev(k)

    def place(g):
        return z if g in Z_FIRST else y

    def owner(g, half):
        where = place(g)
        return device(g, core, lax.rem(where, YL), 2 * x + where // YL, half)

    def is_mine(g, half):
        where = place(g)
        here = jnp.logical_and(yl == lax.rem(where, YL), z == 2 * x + where // YL)
        return jnp.logical_and(jnp.logical_and(x == g, core == half), jnp.logical_and(core == yh, here))

    def owner_slot(g):
        return y if g in Z_FIRST else z

    barrier = pltpu.get_barrier_semaphore()

    def greet(to):
        pl.semaphore_signal(barrier, inc=1, device_id=to, device_id_type=MESH)

    greet({"ctx": nxt, "fsdp": fsdp})
    greet({"ctx": prv, "fsdp": fsdp})
    for k in range(1, 8):
        greet(x_dev(k % 4, k // 4))
        greet(y_dev(k))
        greet(cell_dev(k))
        greet(z_dev(k))
    greeted = 2 + 4 * 7

    def loads(g):
        wide = slice(g * HEADS_W, (g + 1) * HEADS_W)
        lanes = slice(g * HEAD_DIM, (g + 1) * HEAD_DIM)
        return (
            pltpu.make_async_copy(qs.at[0, :, wide], q_v.at[:, wide], loc.at[g, 0]),
            pltpu.make_async_copy(og.at[0, :, wide], g_v.at[:, wide], loc.at[g, 1]),
            pltpu.make_async_copy(ks.at[0, :, lanes], kwin.at[g, 1, 0], loc.at[g, 2]),
            pltpu.make_async_copy(vs.at[0, :, lanes], kwin.at[g, 1, 1], loc.at[g, 3]),
        )

    def hidden_cols(which):
        return hid.at[0, :, pl.ds(pl.multiple_of(which * QUARTER, 128), QUARTER)]

    own_h = pltpu.make_async_copy(hidden_cols(x), hall.at[0], loh)
    for c in loads(0):
        c.start()

    eye = lax.broadcasted_iota(jnp.int32, (TOK, TOK), 0) == lax.broadcasted_iota(jnp.int32, (TOK, TOK), 1)
    own_row = docs[:, pl.ds(pl.multiple_of(ctx * TOK, TOK), TOK)].astype(F32)
    prv_row = docs[:, pl.ds(pl.multiple_of(prv * TOK, TOK), TOK)].astype(F32)
    prv_row = jnp.where(ctx == 0, -1.0, prv_row)

    def as_column(row):
        return jnp.sum(jnp.where(eye, jnp.broadcast_to(row, (TOK, TOK)), 0.0), axis=1, keepdims=True)

    earlier = lax.broadcasted_iota(jnp.int32, (TOK, TOK), 0) <= lax.broadcasted_iota(jnp.int32, (TOK, TOK), 1)
    bias[0:TOK, :] = jnp.where(as_column(prv_row) == own_row, 0.0, -1e30)
    bias[TOK:, :] = jnp.where(jnp.logical_and(as_column(own_row) == own_row, earlier), 0.0, -1e30)

    pl.semaphore_wait(barrier, greeted)

    def window(g):
        lanes = slice(g * HEAD_DIM, (g + 1) * HEAD_DIM)
        to = {"ctx": nxt, "fsdp": fsdp}
        return (
            remote(ks.at[0, :, lanes], kwin.at[g, 0, 0], kvs.at[g], kvr.at[g], to),
            remote(vs.at[0, :, lanes], kwin.at[g, 0, 1], kvs.at[g], kvr.at[g], to),
        )

    for g in range(KV_HEADS):
        for c in window(g):
            c.start()
    for dx in (2, 1, 3):
        remote(hidden_cols(lax.rem(x + dx, X)), hall.at[dx], hs.at[0], hr.at[0], x_dev(dx, 0)).start()
    remote(hidden_cols(x), hall.at[4], hs.at[1], hr.at[1], x_dev(0, 1)).start()
    for g in range(1, KV_HEADS):
        for c in loads(g):
            c.start()
    own_h.start()

    for k in range(1, 8):
        pl.semaphore_signal(word_y, inc=1, device_id=y_dev(k), device_id_type=MESH)

    def pass_word():
        pl.semaphore_wait(word_y, 7)
        for k in range(1, 8):
            pl.semaphore_signal(word_z, inc=1, device_id=z_dev(k), device_id_type=MESH)

    def forward_hidden():
        wait_bytes(hall.at[1:4], hr.at[0])
        for dx in range(1, X):
            remote(hall.at[dx], hall.at[4 + dx], hs.at[1], hr.at[1], x_dev(0, 1)).start()

    def turn_hidden():
        own_h.wait()
        wait_bytes(hall.at[4:8], hr.at[1])
        for k in range(8):
            ht[:, k * TOK:(k + 1) * TOK] = hall[k].T

    scale = 1.0 / math.sqrt(HEAD_DIM)
    scale2 = scale * math.log2(math.e)

    def contrib(g, j):
        return remote(csend.at[g, j], crecv.at[g, j], cs.at[g], cr.at[g], {"ctx": prv, "fsdp": fsdp})

    def attention(g):
        for c in loads(g):
            c.wait()
        wait_bytes(kwin.at[g, 0], kvr.at[g])
        kw = jnp.concatenate([kwin[g, 0, 0], kwin[g, 1, 0]], axis=0)
        vw = jnp.concatenate([kwin[g, 0, 1], kwin[g, 1, 1]], axis=0)
        both = jnp.concatenate([bias[...], bias[...]], axis=1)
        for i in range(GROUP // 2):
            at = [slice((g * GROUP + 2 * i + j) * HEAD_DIM, (g * GROUP + 2 * i + j + 1) * HEAD_DIM) for j in range(2)]
            q2 = jnp.concatenate([q_v[:, at[0]], q_v[:, at[1]]], axis=0)
            g2 = jnp.concatenate([g_v[:, at[0]], g_v[:, at[1]]], axis=0)
            s = mm(kw, q2, ((1,), (1,))) * scale2 + both
            dp = mm(vw, g2, ((1,), (1,)))
            e = jnp.exp2(s - jnp.max(s, axis=0, keepdims=True))
            inv = 1.0 / jnp.sum(e, axis=0, keepdims=True)
            p = e * inv
            delta = jnp.sum(p * dp, axis=0, keepdims=True)
            cols = slice(2 * i * HEAD_DIM, 2 * (i + 1) * HEAD_DIM)
            dsb[:, cols] = (p * (dp - delta)).astype(BF16)
            pbb[:, cols] = p.astype(BF16)
            qst[cols, :] = q2
            gst[cols, :] = g2
        csend[g, 0] = mm(dsb[0:TOK, :], qst[...], ((1,), (0,))) * scale
        contrib(g, 0).start()
        csend[g, 1] = mm(pbb[0:TOK, :], gst[...], ((1,), (0,)))
        contrib(g, 1).start()
        cown[g, 0] = mm(dsb[TOK:, :], qst[...], ((1,), (0,))) * scale
        cown[g, 1] = mm(pbb[TOK:, :], gst[...], ((1,), (0,)))

    def out_copies(g):
        return [
            pltpu.make_async_copy(
                kvb.at[g, j], kv_out.at[0, :, j * KV_W + g * HEAD_DIM:j * KV_W + (g + 1) * HEAD_DIM], outs.at[2 * g + j]
            )
            for j in range(2)
        ]

    def finish(g):
        wait_bytes(crecv.at[g], cr.at[g])
        kvb[g] = (crecv[g] + cown[g]).astype(BF16)
        for k in (2, 6, 1, 3, 5, 7, 4):
            remote(
                kvb.at[g, lax.rem(core + k // 4, 2)], kall.at[g, k], xs.at[g], xr.at[g], x_dev(k % 4, k // 4)
            ).start()
        kall[g, 0] = kvb[g, core]
        for c in out_copies(g):
            c.start()

    def product(g):
        wait_bytes(kall.at[g, 1:8], xr.at[g])
        w = mm(ht[...], kall[g].reshape(8 * TOK, HEAD_DIM), ((1,), (0,))).reshape(Y, CHUNK, HEAD_DIM)
        wlo[g] = w.astype(BF16)
        for k in (4, 3, 5, 2, 6, 1, 7):
            remote(wlo.at[g, lax.rem(place(g) + k, Y)], yrecv.at[g, k], ys.at[g], yr.at[g], first_dev(g, k)).start()
        w32[g] = w

    def z_copy(g, half):
        return remote(zsend.at[g, half], zrecv.at[owner_slot(g)], zs.at[g, half], zr, owner(g, half))

    def y_sum(g):
        wait_bytes(yrecv.at[g, 1:8], yr.at[g])
        total = w32[g, place(g)]
        for k in range(1, Y):
            total = total + yrecv[g, k].astype(F32)
        zsend[g] = total.reshape(2, ROWS, HEAD_DIM)
        for half in range(2):
            mine = is_mine(g, half)

            @pl.when(mine)
            def _(half=half):
                pltpu.make_async_copy(zsend.at[g, half], zrecv.at[owner_slot(g)], zr).start()

            @pl.when(jnp.logical_not(mine))
            def _(half=half):
                z_copy(g, half).start()

    attention(0)
    attention(1)
    finish(0)
    attention(2)
    finish(1)
    forward_hidden()
    attention(3)
    finish(2)
    turn_hidden()
    product(0)
    pass_word()
    product(1)
    finish(3)
    product(2)
    pl.semaphore_wait(word_z, 7)
    y_sum(0)
    product(3)
    y_sum(1)
    y_sum(2)
    y_sum(3)

    wait_bytes(hall.at[1:4], hs.at[0])
    wait_bytes(hall.at[4:8], hs.at[1])
    for g in range(KV_HEADS):
        wait_bytes(kwin.at[g, 0], kvs.at[g])
        wait_bytes(crecv.at[g], cs.at[g])
        wait_bytes(kall.at[g, 1:8], xs.at[g])
        wait_bytes(yrecv.at[g, 1:8], ys.at[g])
        for c in out_copies(g):
            c.wait()
        for half in range(2):
            @pl.when(jnp.logical_not(is_mine(g, half)))
            def _(half=half):
                z_copy(g, half).wait_send()

    wait_bytes(zrecv, zr)
    w = zrecv[0]
    for k in range(1, Z):
        w = w + zrecv[k]

    gpart[...] = mm(w, w, ((0,), (0,)), precision=HIGHEST).reshape(8, 16, HEAD_DIM)
    for k in (6, 7, 4, 5, 2, 3, 1):
        remote(gpart.at[lax.rem(cell + k, 8)], g1buf.at[k], g1s, g1r, cell_dev(k)).start()
    total = gpart[cell]
    wait_bytes(g1buf.at[1:8], g1r)
    for k in range(1, 8):
        total = total + g1buf[k]
    s1[...] = total
    for k in (4, 3, 5, 2, 6, 1, 7):
        remote(s1, g2buf.at[k], g2s, g2r, z_dev(k)).start()
    wait_bytes(g1buf.at[1:8], g1s)
    wait_bytes(g2buf.at[1:8], g2r)
    for k in range(1, 8):
        total = total + g2buf[k]
    gfull[cell] = total
    for k in (6, 7, 4, 5, 2, 3, 1):
        remote(gfull.at[cell], gfull.at[cell], g3s, g3r, cell_dev(k)).start()
    wait_bytes(g2buf.at[1:8], g2s)
    wait_bytes(g1buf.at[1:8], g3r)
    gram = gfull[...].reshape(HEAD_DIM, HEAD_DIM)

    ident = jnp.where(eye, 1.0, 0.0)
    norm = jnp.sqrt(jnp.sum(jnp.sum(gram * ident, axis=1, keepdims=True), axis=0, keepdims=True))
    inv = 1.0 / (norm + 1e-07)
    gram = gram * inv * inv

    def parts(v):
        high = v.astype(BF16)
        rest = v - high.astype(F32)
        mid = rest.astype(BF16)
        return high, mid, (rest - mid.astype(F32)).astype(BF16)

    def left(p):
        return jnp.concatenate([p[2], p[0], p[1], p[1], p[0], p[0]], axis=1)

    def right(p):
        return jnp.concatenate([p[0], p[2], p[1], p[0], p[1], p[0]], axis=0)

    def dot(a, b):
        return mm(a, b, ((1,), (0,)))

    state = w * inv
    for it in range(NS_ITERS):
        gram_parts = parts(gram)
        gram_right = right(gram_parts)
        poly = coeff_a * ident + coeff_b * gram + coeff_c * dot(left(gram_parts), gram_right)
        poly_parts = parts(poly)
        poly_right = right(poly_parts)
        if it < NS_ITERS - 1:
            gram = dot(left(parts(dot(left(poly_parts), gram_right))), poly_right)
        state = dot(left(parts(state)), poly_right)
    up_out[0] = math.sqrt(D) * state
    wait_bytes(g1buf.at[1:8], g3s)


def write_results(kv, up, kv_out, up_out, kv_v, up_v, sems):
    pairs = [(up.at[0], up_v, up_out.at[0], sems.at[4])]
    for i in range(4):
        rows = slice(i * 32, (i + 1) * 32)
        pairs.append((kv.at[0, rows], kv_v.at[rows], kv_out.at[0, rows], sems.at[i]))
    for src, mid, _, sem in pairs:
        pltpu.make_async_copy(src, mid, sem).start()
    for src, mid, dst, sem in pairs:
        pltpu.make_async_copy(src, mid, sem).wait()
        pltpu.make_async_copy(mid, dst, sem).start()
    for _, mid, dst, sem in pairs:
        pltpu.make_async_copy(mid, dst, sem).wait()


def shards(hidden, queries, keys, values, out_grad, doc_ids):
    any_spec = pl.BlockSpec(memory_space=pl.ANY)
    vmem = pl.BlockSpec(memory_space=pltpu.VMEM)
    dma = pltpu.SemaphoreType.DMA
    heads = KV_HEADS
    out_shape = (
        jax.ShapeDtypeStruct((1, TOK, 2 * KV_W), BF16),
        jax.ShapeDtypeStruct((1, ROWS, HEAD_DIM), F32),
    )
    results = pl.pallas_call(
        kernel,
        out_shape=out_shape,
        in_specs=[any_spec] * 5 + [vmem],
        out_specs=(any_spec, vmem),
        scratch_shapes=[
            pltpu.VMEM((TOK, heads * HEADS_W), BF16),
            pltpu.VMEM((TOK, heads * HEADS_W), BF16),
            pltpu.VMEM((heads, 2, 2, TOK, HEAD_DIM), BF16),
            pltpu.VMEM((2 * TOK, TOK), F32),
            pltpu.VMEM((HEADS_W, HEAD_DIM), BF16),
            pltpu.VMEM((HEADS_W, HEAD_DIM), BF16),
            pltpu.VMEM((2 * TOK, HEADS_W), BF16),
            pltpu.VMEM((2 * TOK, HEADS_W), BF16),
            pltpu.VMEM((heads, 2, TOK, HEAD_DIM), F32),
            pltpu.VMEM((heads, 2, TOK, HEAD_DIM), F32),
            pltpu.VMEM((heads, 2, TOK, HEAD_DIM), F32),
            pltpu.VMEM((heads, 2, TOK, HEAD_DIM), BF16),
            pltpu.VMEM((8, TOK, QUARTER), BF16),
            pltpu.VMEM((QUARTER, 8 * TOK), BF16),
            pltpu.VMEM((heads, 8, TOK, HEAD_DIM), BF16),
            pltpu.VMEM((heads, Y, CHUNK, HEAD_DIM), F32),
            pltpu.VMEM((heads, Y, CHUNK, HEAD_DIM), BF16),
            pltpu.VMEM((heads, Y, CHUNK, HEAD_DIM), BF16),
            pltpu.VMEM((heads, 2, ROWS, HEAD_DIM), F32),
            pltpu.VMEM((Z, ROWS, HEAD_DIM), F32),
            pltpu.VMEM((8, 16, HEAD_DIM), F32),
            pltpu.VMEM((8, 16, HEAD_DIM), F32),
            pltpu.VMEM((16, HEAD_DIM), F32),
            pltpu.VMEM((8, 16, HEAD_DIM), F32),
            pltpu.VMEM((8, 16, HEAD_DIM), F32),
            pltpu.SemaphoreType.REGULAR, pltpu.SemaphoreType.REGULAR,
            dma((heads, 4)), dma,
            dma((heads,)), dma((heads,)),
            dma((2,)), dma((2,)),
            dma((heads,)), dma((heads,)),
            dma((heads,)), dma((heads,)),
            dma((heads,)), dma((heads,)),
            dma((heads, 2)), dma,
            dma, dma,
            dma, dma,
            dma, dma,
            dma((2 * heads,)),
        ],
        compiler_params=pltpu.CompilerParams(
            collective_id=0, has_side_effects=True, vmem_limit_bytes=56 * 1024 * 1024
        ),
        name="muon_kv_grads",
    )(hidden, queries, keys, values, out_grad, doc_ids)
    return pl.pallas_call(
        write_results,
        out_shape=out_shape,
        in_specs=[any_spec] * 2,
        out_specs=(any_spec, any_spec),
        scratch_shapes=[
            pltpu.VMEM((TOK, 2 * KV_W), BF16),
            pltpu.VMEM((ROWS, HEAD_DIM), F32),
            dma((5,)),
        ],
        compiler_params=pltpu.CompilerParams(vmem_limit_bytes=56 * 1024 * 1024),
        name="write_results",
    )(*results)


def solution(mesh):
    placed = (P("fsdp", "ctx", None),) * 5 + (P("fsdp", None),)
    return jax.shard_map(
        shards,
        mesh=mesh,
        in_specs=placed,
        out_specs=(P("fsdp", "ctx", None), P("fsdp", "ctx", None)),
        check_vma=False,
    )
```

```python
import math

import jax
import jax.numpy as jnp
from jax import lax
from jax.experimental import pallas as pl
from jax.experimental.pallas import tpu as pltpu
from jax.sharding import PartitionSpec as P

D = 2560
KV_HEADS = 4
GROUP = 12
HEAD_DIM = 128
NS_ITERS = 5
TOK = 128
X, Y, Z, YL = 4, 8, 8, 4
QUARTER = D // X
CHUNK = QUARTER // Y
ROWS = CHUNK // 2
HEADS_W = GROUP * HEAD_DIM
KV_W = KV_HEADS * HEAD_DIM
Z_FIRST = (1,)

coeff_a = 3.4445
coeff_b = -4.775
coeff_c = 2.0315

F32 = jnp.float32
BF16 = jnp.bfloat16
MESH = pl.DeviceIdType.MESH
HIGHEST = lax.Precision.HIGHEST


def device(x, yh, yl, z, core):
    return {"ctx": z * 8 + yl * 2 + core, "fsdp": yh * 4 + x}


def remote(src, dst, send, recv, to):
    return pltpu.make_async_remote_copy(
        src_ref=src, dst_ref=dst, send_sem=send, recv_sem=recv, device_id=to, device_id_type=MESH
    )


def mm(a, b, dims, **kw):
    return lax.dot_general(a, b, ((dims[0], dims[1]), ((), ())), preferred_element_type=F32, **kw)


def wait_bytes(ref, sem):
    pltpu.make_async_copy(ref, ref, sem).wait()


def kernel(
    hid, qs, ks, vs, og, docs, kv_out, up_out,
    q_v, g_v, kwin, bias, qst, gst, dsb, pbb, csend, cown, crecv, kvb, hall, ht, kall, w32, wlo,
    yrecv, zsend, zrecv, gpart, g1buf, s1, g2buf, gfull,
    word_y, word_z, loc, loh, kvs, kvr, hs, hr, cs, cr, xs, xr, ys, yr, zs, zr, g1s, g1r, g2s, g2r, g3s, g3r, outs,
):
    ctx, fsdp = lax.axis_index("ctx"), lax.axis_index("fsdp")
    z, yl, core = ctx // 8, lax.rem(ctx // 2, YL), lax.rem(ctx, 2)
    yh, x = fsdp // X, lax.rem(fsdp, X)
    y = yh * YL + yl
    cell = yl * 2 + core
    nxt, prv = lax.rem(ctx + 1, 64), lax.rem(ctx + 63, 64)

    def x_dev(dx, dc):
        return device(lax.rem(x + dx, X), yh, yl, z, lax.rem(core + dc, 2))

    def y_dev(k):
        to = lax.rem(y + k, Y)
        return device(x, to // YL, lax.rem(to, YL), z, core)

    def cell_dev(k):
        return {"ctx": z * 8 + lax.rem(cell + k, 8), "fsdp": fsdp}

    def z_dev(k):
        return {"ctx": lax.rem(z + k, Z) * 8 + cell, "fsdp": fsdp}

    def first_dev(g, k):
        return z_dev(k) if g in Z_FIRST else y_dev(k)

    def place(g):
        return z if g in Z_FIRST else y

    def owner(g, half):
        where = place(g)
        return device(g, core, lax.rem(where, YL), 2 * x + where // YL, half)

    def is_mine(g, half):
        where = place(g)
        here = jnp.logical_and(yl == lax.rem(where, YL), z == 2 * x + where // YL)
        return jnp.logical_and(jnp.logical_and(x == g, core == half), jnp.logical_and(core == yh, here))

    def owner_slot(g):
        return y if g in Z_FIRST else z

    barrier = pltpu.get_barrier_semaphore()

    def greet(to):
        pl.semaphore_signal(barrier, inc=1, device_id=to, device_id_type=MESH)

    greet({"ctx": nxt, "fsdp": fsdp})
    greet({"ctx": prv, "fsdp": fsdp})
    for k in range(1, 8):
        greet(x_dev(k % 4, k // 4))
        greet(y_dev(k))
        greet(cell_dev(k))
        greet(z_dev(k))
    greeted = 2 + 4 * 7

    def loads(g):
        wide = slice(g * HEADS_W, (g + 1) * HEADS_W)
        lanes = slice(g * HEAD_DIM, (g + 1) * HEAD_DIM)
        return (
            pltpu.make_async_copy(qs.at[0, :, wide], q_v.at[:, wide], loc.at[g, 0]),
            pltpu.make_async_copy(og.at[0, :, wide], g_v.at[:, wide], loc.at[g, 1]),
            pltpu.make_async_copy(ks.at[0, :, lanes], kwin.at[g, 1, 0], loc.at[g, 2]),
            pltpu.make_async_copy(vs.at[0, :, lanes], kwin.at[g, 1, 1], loc.at[g, 3]),
        )

    def hidden_cols(which):
        return hid.at[0, :, pl.ds(pl.multiple_of(which * QUARTER, 128), QUARTER)]

    own_h = pltpu.make_async_copy(hidden_cols(x), hall.at[0], loh)
    for c in loads(0):
        c.start()

    eye = lax.broadcasted_iota(jnp.int32, (TOK, TOK), 0) == lax.broadcasted_iota(jnp.int32, (TOK, TOK), 1)
    own_row = docs[:, pl.ds(pl.multiple_of(ctx * TOK, TOK), TOK)].astype(F32)
    prv_row = docs[:, pl.ds(pl.multiple_of(prv * TOK, TOK), TOK)].astype(F32)
    prv_row = jnp.where(ctx == 0, -1.0, prv_row)

    def as_column(row):
        return jnp.sum(jnp.where(eye, jnp.broadcast_to(row, (TOK, TOK)), 0.0), axis=1, keepdims=True)

    earlier = lax.broadcasted_iota(jnp.int32, (TOK, TOK), 0) <= lax.broadcasted_iota(jnp.int32, (TOK, TOK), 1)
    bias[0:TOK, :] = jnp.where(as_column(prv_row) == own_row, 0.0, -1e30)
    bias[TOK:, :] = jnp.where(jnp.logical_and(as_column(own_row) == own_row, earlier), 0.0, -1e30)

    pl.semaphore_wait(barrier, greeted)

    def window(g):
        lanes = slice(g * HEAD_DIM, (g + 1) * HEAD_DIM)
        to = {"ctx": nxt, "fsdp": fsdp}
        return (
            remote(ks.at[0, :, lanes], kwin.at[g, 0, 0], kvs.at[g], kvr.at[g], to),
            remote(vs.at[0, :, lanes], kwin.at[g, 0, 1], kvs.at[g], kvr.at[g], to),
        )

    for g in range(KV_HEADS):
        for c in window(g):
            c.start()
    for dx in (2, 1, 3):
        remote(hidden_cols(lax.rem(x + dx, X)), hall.at[dx], hs.at[0], hr.at[0], x_dev(dx, 0)).start()
    remote(hidden_cols(x), hall.at[4], hs.at[1], hr.at[1], x_dev(0, 1)).start()
    for g in range(1, KV_HEADS):
        for c in loads(g):
            c.start()
    own_h.start()

    for k in range(1, 8):
        pl.semaphore_signal(word_y, inc=1, device_id=y_dev(k), device_id_type=MESH)

    def pass_word():
        pl.semaphore_wait(word_y, 7)
        for k in range(1, 8):
            pl.semaphore_signal(word_z, inc=1, device_id=z_dev(k), device_id_type=MESH)

    def forward_hidden():
        wait_bytes(hall.at[1:4], hr.at[0])
        for dx in range(1, X):
            remote(hall.at[dx], hall.at[4 + dx], hs.at[1], hr.at[1], x_dev(0, 1)).start()

    def turn_hidden():
        own_h.wait()
        wait_bytes(hall.at[4:8], hr.at[1])
        for k in range(8):
            ht[:, k * TOK:(k + 1) * TOK] = hall[k].T

    scale = 1.0 / math.sqrt(HEAD_DIM)
    scale2 = scale * math.log2(math.e)

    def contrib(g, j):
        return remote(csend.at[g, j], crecv.at[g, j], cs.at[g], cr.at[g], {"ctx": prv, "fsdp": fsdp})

    def attention(g):
        for c in loads(g):
            c.wait()
        wait_bytes(kwin.at[g, 0], kvr.at[g])
        kw = jnp.concatenate([kwin[g, 0, 0], kwin[g, 1, 0]], axis=0)
        vw = jnp.concatenate([kwin[g, 0, 1], kwin[g, 1, 1]], axis=0)
        both = jnp.concatenate([bias[...], bias[...]], axis=1)
        for i in range(GROUP // 2):
            at = [slice((g * GROUP + 2 * i + j) * HEAD_DIM, (g * GROUP + 2 * i + j + 1) * HEAD_DIM) for j in range(2)]
            q2 = jnp.concatenate([q_v[:, at[0]], q_v[:, at[1]]], axis=0)
            g2 = jnp.concatenate([g_v[:, at[0]], g_v[:, at[1]]], axis=0)
            s = mm(kw, q2, ((1,), (1,))) * scale2 + both
            dp = mm(vw, g2, ((1,), (1,)))
            e = jnp.exp2(s - jnp.max(s, axis=0, keepdims=True))
            inv = 1.0 / jnp.sum(e, axis=0, keepdims=True)
            p = e * inv
            delta = jnp.sum(p * dp, axis=0, keepdims=True)
            cols = slice(2 * i * HEAD_DIM, 2 * (i + 1) * HEAD_DIM)
            dsb[:, cols] = (p * (dp - delta)).astype(BF16)
            pbb[:, cols] = p.astype(BF16)
            qst[cols, :] = q2
            gst[cols, :] = g2
        csend[g, 0] = (mm(dsb[0:TOK, :], qst[...], ((1,), (0,))) * scale).astype(BF16)
        contrib(g, 0).start()
        csend[g, 1] = mm(pbb[0:TOK, :], gst[...], ((1,), (0,))).astype(BF16)
        contrib(g, 1).start()
        cown[g, 0] = mm(dsb[TOK:, :], qst[...], ((1,), (0,))) * scale
        cown[g, 1] = mm(pbb[TOK:, :], gst[...], ((1,), (0,)))

    def out_copies(g):
        return [
            pltpu.make_async_copy(
                kvb.at[g, j], kv_out.at[0, :, j * KV_W + g * HEAD_DIM:j * KV_W + (g + 1) * HEAD_DIM], outs.at[2 * g + j]
            )
            for j in range(2)
        ]

    def finish(g):
        wait_bytes(crecv.at[g], cr.at[g])
        kvb[g] = (crecv[g].astype(F32) + cown[g]).astype(BF16)
        for k in (2, 6, 1, 3, 5, 7, 4):
            remote(
                kvb.at[g, lax.rem(core + k // 4, 2)], kall.at[g, k], xs.at[g], xr.at[g], x_dev(k % 4, k // 4)
            ).start()
        kall[g, 0] = kvb[g, core]
        for c in out_copies(g):
            c.start()

    def product(g):
        wait_bytes(kall.at[g, 1:8], xr.at[g])
        w = mm(ht[...], kall[g].reshape(8 * TOK, HEAD_DIM), ((1,), (0,))).reshape(Y, CHUNK, HEAD_DIM)
        wlo[g] = w.astype(BF16)
        for k in (4, 3, 5, 2, 6, 1, 7):
            remote(wlo.at[g, lax.rem(place(g) + k, Y)], yrecv.at[g, k], ys.at[g], yr.at[g], first_dev(g, k)).start()
        w32[g] = w

    def z_copy(g, half):
        return remote(zsend.at[g, half], zrecv.at[owner_slot(g)], zs.at[g, half], zr, owner(g, half))

    def y_sum(g):
        wait_bytes(yrecv.at[g, 1:8], yr.at[g])
        total = w32[g, place(g)]
        for k in range(1, Y):
            total = total + yrecv[g, k].astype(F32)
        zsend[g] = total.reshape(2, ROWS, HEAD_DIM)
        for half in range(2):
            mine = is_mine(g, half)

            @pl.when(mine)
            def _(half=half):
                pltpu.make_async_copy(zsend.at[g, half], zrecv.at[owner_slot(g)], zr).start()

            @pl.when(jnp.logical_not(mine))
            def _(half=half):
                z_copy(g, half).start()

    attention(0)
    attention(1)
    finish(0)
    attention(2)
    finish(1)
    forward_hidden()
    attention(3)
    finish(2)
    turn_hidden()
    product(0)
    pass_word()
    product(1)
    finish(3)
    product(2)
    pl.semaphore_wait(word_z, 7)
    y_sum(0)
    product(3)
    y_sum(1)
    y_sum(2)
    y_sum(3)

    wait_bytes(hall.at[1:4], hs.at[0])
    wait_bytes(hall.at[4:8], hs.at[1])
    for g in range(KV_HEADS):
        wait_bytes(kwin.at[g, 0], kvs.at[g])
        wait_bytes(crecv.at[g], cs.at[g])
        wait_bytes(kall.at[g, 1:8], xs.at[g])
        wait_bytes(yrecv.at[g, 1:8], ys.at[g])
        for c in out_copies(g):
            c.wait()
        for half in range(2):
            @pl.when(jnp.logical_not(is_mine(g, half)))
            def _(half=half):
                z_copy(g, half).wait_send()

    wait_bytes(zrecv, zr)
    w = zrecv[0]
    for k in range(1, Z):
        w = w + zrecv[k]

    gpart[...] = mm(w, w, ((0,), (0,)), precision=HIGHEST).reshape(8, 16, HEAD_DIM)
    for k in (6, 7, 4, 5, 2, 3, 1):
        remote(gpart.at[lax.rem(cell + k, 8)], g1buf.at[k], g1s, g1r, cell_dev(k)).start()
    total = gpart[cell]
    wait_bytes(g1buf.at[1:8], g1r)
    for k in range(1, 8):
        total = total + g1buf[k]
    s1[...] = total
    for k in (4, 3, 5, 2, 6, 1, 7):
        remote(s1, g2buf.at[k], g2s, g2r, z_dev(k)).start()
    wait_bytes(g1buf.at[1:8], g1s)
    wait_bytes(g2buf.at[1:8], g2r)
    for k in range(1, 8):
        total = total + g2buf[k]
    gfull[cell] = total
    for k in (6, 7, 4, 5, 2, 3, 1):
        remote(gfull.at[cell], gfull.at[cell], g3s, g3r, cell_dev(k)).start()
    wait_bytes(g2buf.at[1:8], g2s)
    wait_bytes(g1buf.at[1:8], g3r)
    gram = gfull[...].reshape(HEAD_DIM, HEAD_DIM)

    ident = jnp.where(eye, 1.0, 0.0)
    norm = jnp.sqrt(jnp.sum(jnp.sum(gram * ident, axis=1, keepdims=True), axis=0, keepdims=True))
    inv = 1.0 / (norm + 1e-07)
    gram = gram * inv * inv

    def parts(v):
        high = v.astype(BF16)
        rest = v - high.astype(F32)
        mid = rest.astype(BF16)
        return high, mid, (rest - mid.astype(F32)).astype(BF16)

    def left(p):
        return jnp.concatenate([p[2], p[0], p[1], p[1], p[0], p[0]], axis=1)

    def right(p):
        return jnp.concatenate([p[0], p[2], p[1], p[0], p[1], p[0]], axis=0)

    def dot(a, b):
        return mm(a, b, ((1,), (0,)))

    state = w * inv
    for it in range(NS_ITERS):
        gram_parts = parts(gram)
        gram_right = right(gram_parts)
        poly = coeff_a * ident + coeff_b * gram + coeff_c * dot(left(gram_parts), gram_right)
        poly_parts = parts(poly)
        poly_right = right(poly_parts)
        if it < NS_ITERS - 1:
            gram = dot(left(parts(dot(left(poly_parts), gram_right))), poly_right)
        state = dot(left(parts(state)), poly_right)
    up_out[0] = math.sqrt(D) * state
    wait_bytes(g1buf.at[1:8], g3s)


def write_results(kv, up, kv_out, up_out, kv_v, up_v, sems):
    pairs = [(up.at[0], up_v, up_out.at[0], sems.at[4])]
    for i in range(4):
        rows = slice(i * 32, (i + 1) * 32)
        pairs.append((kv.at[0, rows], kv_v.at[rows], kv_out.at[0, rows], sems.at[i]))
    for src, mid, _, sem in pairs:
        pltpu.make_async_copy(src, mid, sem).start()
    for src, mid, dst, sem in pairs:
        pltpu.make_async_copy(src, mid, sem).wait()
        pltpu.make_async_copy(mid, dst, sem).start()
    for _, mid, dst, sem in pairs:
        pltpu.make_async_copy(mid, dst, sem).wait()


def shards(hidden, queries, keys, values, out_grad, doc_ids):
    any_spec = pl.BlockSpec(memory_space=pl.ANY)
    vmem = pl.BlockSpec(memory_space=pltpu.VMEM)
    dma = pltpu.SemaphoreType.DMA
    heads = KV_HEADS
    out_shape = (
        jax.ShapeDtypeStruct((1, TOK, 2 * KV_W), BF16),
        jax.ShapeDtypeStruct((1, ROWS, HEAD_DIM), F32),
    )
    results = pl.pallas_call(
        kernel,
        out_shape=out_shape,
        in_specs=[any_spec] * 5 + [vmem],
        out_specs=(any_spec, vmem),
        scratch_shapes=[
            pltpu.VMEM((TOK, heads * HEADS_W), BF16),
            pltpu.VMEM((TOK, heads * HEADS_W), BF16),
            pltpu.VMEM((heads, 2, 2, TOK, HEAD_DIM), BF16),
            pltpu.VMEM((2 * TOK, TOK), F32),
            pltpu.VMEM((HEADS_W, HEAD_DIM), BF16),
            pltpu.VMEM((HEADS_W, HEAD_DIM), BF16),
            pltpu.VMEM((2 * TOK, HEADS_W), BF16),
            pltpu.VMEM((2 * TOK, HEADS_W), BF16),
            pltpu.VMEM((heads, 2, TOK, HEAD_DIM), BF16),
            pltpu.VMEM((heads, 2, TOK, HEAD_DIM), F32),
            pltpu.VMEM((heads, 2, TOK, HEAD_DIM), BF16),
            pltpu.VMEM((heads, 2, TOK, HEAD_DIM), BF16),
            pltpu.VMEM((8, TOK, QUARTER), BF16),
            pltpu.VMEM((QUARTER, 8 * TOK), BF16),
            pltpu.VMEM((heads, 8, TOK, HEAD_DIM), BF16),
            pltpu.VMEM((heads, Y, CHUNK, HEAD_DIM), F32),
            pltpu.VMEM((heads, Y, CHUNK, HEAD_DIM), BF16),
            pltpu.VMEM((heads, Y, CHUNK, HEAD_DIM), BF16),
            pltpu.VMEM((heads, 2, ROWS, HEAD_DIM), F32),
            pltpu.VMEM((Z, ROWS, HEAD_DIM), F32),
            pltpu.VMEM((8, 16, HEAD_DIM), F32),
            pltpu.VMEM((8, 16, HEAD_DIM), F32),
            pltpu.VMEM((16, HEAD_DIM), F32),
            pltpu.VMEM((8, 16, HEAD_DIM), F32),
            pltpu.VMEM((8, 16, HEAD_DIM), F32),
            pltpu.SemaphoreType.REGULAR, pltpu.SemaphoreType.REGULAR,
            dma((heads, 4)), dma,
            dma((heads,)), dma((heads,)),
            dma((2,)), dma((2,)),
            dma((heads,)), dma((heads,)),
            dma((heads,)), dma((heads,)),
            dma((heads,)), dma((heads,)),
            dma((heads, 2)), dma,
            dma, dma,
            dma, dma,
            dma, dma,
            dma((2 * heads,)),
        ],
        compiler_params=pltpu.CompilerParams(
            collective_id=0, has_side_effects=True, vmem_limit_bytes=56 * 1024 * 1024
        ),
        name="muon_kv_grads",
    )(hidden, queries, keys, values, out_grad, doc_ids)
    return pl.pallas_call(
        write_results,
        out_shape=out_shape,
        in_specs=[any_spec] * 2,
        out_specs=(any_spec, any_spec),
        scratch_shapes=[
            pltpu.VMEM((TOK, 2 * KV_W), BF16),
            pltpu.VMEM((ROWS, HEAD_DIM), F32),
            dma((5,)),
        ],
        compiler_params=pltpu.CompilerParams(vmem_limit_bytes=56 * 1024 * 1024),
        name="write_results",
    )(*results)


def solution(mesh):
    placed = (P("fsdp", "ctx", None),) * 5 + (P("fsdp", None),)
    return jax.shard_map(
        shards,
        mesh=mesh,
        in_specs=placed,
        out_specs=(P("fsdp", "ctx", None), P("fsdp", "ctx", None)),
        check_vma=False,
    )
```
